128 devices in a mesh: dp: 16 (over z, x), tensor: 8 (over y, core).
Axes of the slice: x: 4, y: 4, z: 4, core: 2. Of those that a mesh axis runs over, the one named last changes fastest.
Arguments:
- hidden: bfloat16 [2048, 8192], P(('dp', 'tensor')), may hold values from -400 to 400
- gain: float32 [8192], replicated, may hold values from 0.5 to 1.5
- w_query: bfloat16 [8192, 8192], P(None, 'tensor'), may hold values from -16 to 16
- w_key: bfloat16 [8192, 1024], P(None, 'tensor'), may hold values from -1 to 1
- w_value: bfloat16 [8192, 1024], P(None, 'tensor'), may hold values from -0.0625 to 0.0625
- out_grad: bfloat16 [2048, 8192], P(('dp', 'tensor')), may hold values from -6 to 6
- owner: int32 [2048, 1], P(('dp', 'tensor')), may hold values from 0 to 15; in each aligned block of 16 rows (0 to 15, 16 to 31, ...) at most 2 rows name the same one
- completion: int32 [2048], P(('dp', 'tensor')), may hold values from 0 to 15
- rewards: int32 [16, 16], P('dp'), may hold values from -512 to 511
Outputs:
- grad_hidden: bfloat16 [2048, 8192], P(('dp', 'tensor'))
The draws below stay inside these ranges and needn't reach their ends.
Inputs may be any that keep to these rules, and one draw needn't show every extreme that they name: Among the rows of one device, one owner group is named at most 2 times; in every draw some device names some group exactly 2 times. Fixed-point rewards in units of 1/256.
All inputs are finite; a program needn't handle non-finite values.
Results may differ from the reference program's by a relative error of at most 0.015.
Values may be sent and summed in bfloat16 or wider, within the bound.
No kernel may reach another device: no remote copies, remote signals or barrier semaphores. Data moves between devices by JAX's collectives and lax.ppermute only.
A program may use at most 128 MiB of HBM per device.

```python
import math
import jax
import jax.numpy as jnp
import numpy as np
from jax import lax

D = 8192
HEADS = 64
KV = 8
HD = 128
KC = 16
GEN_ROWS = 16
CAP = 2
SLOTS = 256
ALL_ROWS = 2048
N_DP = 16
N_TENSOR = 8


def shared_keys(key):
    return jnp.clip(jax.random.normal(key, (D, KV * HD), jnp.float32), -4.0, 4.0)


def draw_w_key(key, part):
    shared = shared_keys(key)
    return (shared * D ** (-0.5)).astype(jnp.bfloat16)


def draw_w_query(key, part):
    key = jax.random.fold_in(key, 12)
    own = jnp.clip(jax.random.normal(key, (D, HEADS * HD), jnp.float32), -4.0, 4.0)
    return (own * D ** (-0.5)).astype(jnp.bfloat16)


def draw_hidden(key, part):
    key = jax.random.fold_in(key, 13)
    first, second, third = jax.random.split(key, 3)
    row_scale = jnp.exp(jax.random.uniform(first, (ALL_ROWS, 1), jnp.float32, 0.0, 2.3))
    col_scale = jnp.exp(jax.random.uniform(second, (1, D), jnp.float32, 0.0, 2.3))
    base = jnp.clip(jax.random.normal(third, (ALL_ROWS, D), jnp.float32), -4.0, 4.0)
    return (base * row_scale * col_scale).astype(jnp.bfloat16)


def with_ends(entries, rng, low, largest):
    spot = [jax.random.randint(jax.random.fold_in(rng, axis), (), 0, length) for axis, length in enumerate(entries.shape)]
    widest = entries.shape.index(max(entries.shape))
    neighbour = spot[:widest] + [(spot[widest] + 1) % entries.shape[widest]] + spot[widest + 1:]
    return entries.at[tuple(spot)].set(low).at[tuple(neighbour)].set(largest)


def block_scale(key, shape, shards, low, top_value):
    loudness, own = 1.0, jax.random.fold_in(key, 6)
    for axis_at, blocks in shards:
        draws = jnp.exp(jax.random.uniform(jax.random.fold_in(own, axis_at), (blocks,), jnp.float32, low / len(shards), top_value / len(shards)))
        loudness = loudness * jnp.repeat(draws, shape[axis_at] // blocks).reshape([-1 if axis == axis_at else 1 for axis in range(len(shape))])
    return loudness


def shared_out(rng, own, number, rows, number_of, top, limit, skew):
    ranking = jax.random.permutation(rng, number_of)
    packed, ordinary = shares(number_of, rows * top, limit, skew, True), shares(number_of, rows * top, limit, skew, False)
    places = jnp.arange(number_of)

    def named(sizes, offset_by):
        used = int((sizes > 0).sum())
        fixed = max(1, used // 4)
        passed = fixed + (places - fixed + offset_by * (used - fixed)) % max(1, number_of - fixed)
        return jnp.zeros((number_of,), jnp.int32).at[ranking[jnp.where(places < fixed, places, passed)]].set(jnp.asarray(sizes, jnp.int32))

    sizes = jnp.where(number % 4 == 0, named(packed, number // 4), named(ordinary, number - number // 4 - 1))
    mixed = jax.random.permutation(jax.random.fold_in(own, 3), number_of)
    source_of, receiver = mixed[0:number_of // 2 * 2:2], mixed[1:number_of // 2 * 2:2]
    margin = jnp.minimum(sizes[source_of] - 1, limit - sizes[receiver]) // 2
    margin = jnp.where((source_of == ranking[0]) | (receiver == ranking[0]) | (sizes[receiver] == 0), 0, jnp.maximum(margin, 0))
    passed = jax.random.randint(jax.random.fold_in(own, 4), (number_of // 2,), 0, 1 << 20) % (margin + 1)
    sizes = sizes.at[source_of].add(-passed).at[receiver].add(passed)
    members = jnp.searchsorted(jnp.cumsum(sizes), jnp.arange(rows * top), side="right").astype(jnp.int32)
    listing = members.reshape(top, rows).T
    listing = listing[jax.random.permutation(jax.random.fold_in(own, 1), rows)]
    offset_by = jax.random.randint(jax.random.fold_in(own, 2), (rows, 1), 0, top)
    return jnp.take_along_axis(listing, (jnp.arange(top)[None, :] + offset_by) % top, axis=1)


def shares(number_of, total, reach, slope, full):
    loads = [(1 << 20) // math.isqrt(grade ** slope) + 1 for grade in range(1, number_of + 1)]
    largest = reach if full else min(reach, max(-(-total // number_of), total * loads[0] // sum(loads)))
    least = 1 if total - largest >= number_of - 1 else 0
    counts, rest = [largest] + [least] * (number_of - 1), total - largest - least * (number_of - 1)
    while rest > 0:
        movable = [i for i in range(1, number_of) if counts[i] < largest] or [i for i in range(1, number_of) if counts[i] < reach]
        whole, budget = sum([loads[i] for i in movable]), rest
        for i in movable:
            addition = min(reach - counts[i], max(1, budget * loads[i] // whole), rest)
            counts[i] = counts[i] + addition
            rest = rest - addition
    return np.array(counts)


def centred(own_key, shape, spread, most, cuts=(), held_as=jnp.bfloat16):
    level = block_scale(own_key, shape, cuts, -0.22, 0.18) if cuts else 1.0
    values = jax.random.normal(own_key, shape, jnp.float32) * spread * level
    return jnp.minimum(jnp.maximum(values, -most), most).astype(held_as)


def setup_inputs(seed: int = 0) -> dict:
    streams_of = jax.random.split(jax.random.key(seed), 10)
    hidden = draw_hidden(jax.random.fold_in(streams_of[9], 71), 0)
    gain = jnp.clip(1.0 + 0.1 * jax.random.normal(streams_of[1], (D,), jnp.float32), 0.5, 1.5)
    w_query = draw_w_query(jax.random.fold_in(streams_of[9], 71), 0)
    w_key = draw_w_key(jax.random.fold_in(streams_of[9], 71), 0)
    w_value = centred(streams_of[4], (D, KV * HD), D ** -0.5, 0.0625, ((1, 8),))
    out_grad = centred(streams_of[5], (ALL_ROWS, HEADS * HD), 1.0, 6.0, ((0, 128),))
    owner_keys = jax.random.split(jax.random.fold_in(streams_of[6], 1), ALL_ROWS // GEN_ROWS)
    owner_turns = jax.random.permutation(jax.random.fold_in(streams_of[6], 3), ALL_ROWS // GEN_ROWS)
    owner = jax.vmap(lambda own, number: shared_out(jax.random.fold_in(streams_of[6], 2), own, number, GEN_ROWS, N_DP, 1, CAP, 2))(owner_keys, owner_turns).reshape((ALL_ROWS, 1))
    completion = with_ends(jax.random.randint(streams_of[7], (ALL_ROWS,), 0, KC), jax.random.fold_in(streams_of[7], 1), 0, KC - 1).astype(jnp.int32)
    rewards = with_ends(jax.random.randint(streams_of[8], (N_DP, KC), -512, 512), jax.random.fold_in(streams_of[8], 1), -512, 511).astype(jnp.int32)
    return dict(hidden=hidden, gain=gain, w_query=w_query, w_key=w_key, w_value=w_value, out_grad=out_grad, owner=owner, completion=completion, rewards=rewards)


epsilon = 1e-05
base_freq = 500000.0

def angles(position, size):
    half = size // 2
    freq = base_freq ** (-2.0 * jnp.arange(half, dtype=jnp.float32) / size)
    angle = position.astype(jnp.float32)[:, None] * freq[None, :]
    return (jnp.cos(angle), jnp.sin(angle))

def rotate(values, cosine, sine):
    half = values.shape[-1] // 2
    first = values[..., :half]
    second = values[..., half:]
    return jnp.concatenate([first * cosine - second * sine, second * cosine + first * sine], axis=-1)

def attend_back(query, keys, values, grad_head, labels, order):
    size = query.shape[-1]
    factor = size ** (-0.5)
    allowed = (labels[:, None] == labels[None, :]) & (order[None, :] <= order[:, None])
    query_wide = query.astype(jnp.float32)
    keys_wide = keys.astype(jnp.float32)
    values_wide = values.astype(jnp.float32)
    grad_wide = grad_head.astype(jnp.float32)
    scores = jnp.einsum('gpqd,gkd->gpqk', query_wide, keys_wide) * factor
    scores = jnp.where(allowed, scores, -1e+30)
    highest = lax.optimization_barrier(jnp.max(scores, axis=-1, keepdims=True))
    weights = jnp.exp(scores - highest)
    probs = weights / lax.optimization_barrier(jnp.sum(weights, axis=-1, keepdims=True))
    rounded_probs = lax.optimization_barrier(probs.astype(jnp.bfloat16)).astype(jnp.float32)
    grad_value = jnp.einsum('gpqk,gpqd->gkd', rounded_probs, grad_wide).astype(jnp.bfloat16)
    grad_probs = jnp.einsum('gpqd,gkd->gpqk', grad_wide, values_wide)
    inner = lax.optimization_barrier(jnp.sum(probs * grad_probs, axis=-1, keepdims=True))
    grad_scores = (probs * (grad_probs - inner) * factor).astype(jnp.bfloat16)
    grad_scores = lax.optimization_barrier(grad_scores).astype(jnp.float32)
    grad_query = jnp.einsum('gpqk,gkd->gpqd', grad_scores, keys_wide)
    grad_key = jnp.einsum('gpqk,gpqd->gkd', grad_scores, query_wide)
    return (grad_query, grad_key, grad_value)

def reference(hidden, gain, w_query, w_key, w_value, out_grad, owner, completion, rewards):
    total, width = hidden.shape
    groups = N_DP
    slots = SLOTS
    share = HEADS // KV
    wide = hidden.astype(jnp.float32)
    inverse = lax.rsqrt(lax.optimization_barrier(jnp.mean(wide * wide, axis=1, keepdims=True)) + epsilon)
    normed = (wide * inverse * gain[None, :]).astype(jnp.bfloat16)
    target = owner[:, 0]
    member = (target[:, None] == jnp.arange(groups, dtype=jnp.int32)[None, :]).astype(jnp.int32)
    slot_rank = lax.optimization_barrier(jnp.sum((jnp.cumsum(member, axis=0) - member) * member, axis=1)).astype(jnp.int32)
    owner_label = target * KC + completion
    matches = (owner_label[:, None] == jnp.arange(groups * KC, dtype=jnp.int32)[None, :]).astype(jnp.int32)
    position = lax.optimization_barrier(jnp.sum((jnp.cumsum(matches, axis=0) - matches) * matches, axis=1)).astype(jnp.int32)
    slot_index = (target * slots + slot_rank).astype(jnp.int32)
    table = jnp.full((groups * slots,), total, jnp.int32).at[slot_index].set(jnp.arange(total, dtype=jnp.int32))
    filled = table < total
    clipped = jnp.minimum(table, total - 1).astype(jnp.int32)
    cosine, sine = angles(position, HD)
    cosine = cosine[:, None, :]
    sine = sine[:, None, :]
    query = rotate(jnp.dot(normed, w_query, preferred_element_type=jnp.float32).reshape(total, HEADS, HD), cosine, sine).astype(jnp.bfloat16)
    keys = rotate(jnp.dot(normed, w_key, preferred_element_type=jnp.float32).reshape(total, KV, HD), cosine, sine).astype(jnp.bfloat16)
    values = jnp.dot(normed, w_value, preferred_element_type=jnp.float32).astype(jnp.bfloat16).reshape(total, KV, HD)
    scaled = rewards.astype(jnp.float32) / 256.0
    advantage = scaled - (lax.optimization_barrier(jnp.sum(scaled, axis=1, keepdims=True)) - scaled) / (KC - 1)
    row_weight = advantage[target, completion]
    grad_head = (out_grad.astype(jnp.float32) * row_weight[:, None]).astype(jnp.bfloat16).reshape(total, HEADS, HD)

    def one_group(index):
        picked = lax.dynamic_slice_in_dim(clipped, (index * slots).astype(jnp.int32), slots)
        live = lax.dynamic_slice_in_dim(filled, (index * slots).astype(jnp.int32), slots)
        labels = jnp.where(live, completion[picked], -1)
        order = jnp.where(live, position[picked], 0)
        live3 = live[:, None, None]
        group_query = jnp.where(live3, query[picked], 0).transpose(1, 0, 2).reshape(KV, share, slots, HD)
        group_keys = jnp.where(live3, keys[picked], 0).transpose(1, 0, 2)
        group_values = jnp.where(live3, values[picked], 0).transpose(1, 0, 2)
        group_grad = jnp.where(live3, grad_head[picked], 0).transpose(1, 0, 2).reshape(KV, share, slots, HD)
        grad_query, grad_key, grad_value = attend_back(group_query, group_keys, group_values, group_grad, labels, order)
        return (grad_query.reshape(HEADS, slots, HD).transpose(1, 0, 2), grad_key.transpose(1, 0, 2), grad_value.transpose(1, 0, 2))
    query_all, key_all, value_all = lax.map(one_group, jnp.arange(groups, dtype=jnp.int32))
    query_rows = query_all.reshape(groups * slots, HEADS, HD)[slot_index]
    key_rows = key_all.reshape(groups * slots, KV, HD)[slot_index]
    value_rows = value_all.reshape(groups * slots, KV, HD)[slot_index]
    back_query = rotate(query_rows, cosine, -sine).astype(jnp.bfloat16).reshape(total, HEADS * HD)
    back_key = rotate(key_rows, cosine, -sine).astype(jnp.bfloat16).reshape(total, KV * HD)
    back_value = value_rows.reshape(total, KV * HD)
    query_span = HEADS * HD // N_TENSOR
    key_span = KV * HD // N_TENSOR
    grad_normed = jnp.zeros((total, width), jnp.float32)
    for part_index in range(N_TENSOR):
        query_cols = slice(part_index * query_span, (part_index + 1) * query_span)
        key_cols = slice(part_index * key_span, (part_index + 1) * key_span)
        group_term = jnp.dot(back_query[:, query_cols], w_query[:, query_cols].T, preferred_element_type=jnp.float32)
        group_term = group_term + jnp.dot(back_key[:, key_cols], w_key[:, key_cols].T, preferred_element_type=jnp.float32)
        group_term = group_term + jnp.dot(back_value[:, key_cols], w_value[:, key_cols].T, preferred_element_type=jnp.float32)
        grad_normed = grad_normed + lax.optimization_barrier(group_term.astype(jnp.bfloat16)).astype(jnp.float32)
    scaled_grad = grad_normed * gain[None, :]
    inner = lax.optimization_barrier(jnp.mean(scaled_grad * wide, axis=1, keepdims=True))
    return (inverse * scaled_grad - wide * inverse * inverse * inverse * inner).astype(jnp.bfloat16)
```

```python
import jax
import jax.numpy as jnp
from jax import lax
from jax.experimental import pallas as pl
from jax.experimental.pallas import tpu as pltpu
from jax.sharding import PartitionSpec as P

HD = 128
KC = 16
PARTS = 2
EXT = 128
STEP = 1024
EPSILON = 1e-05
BASE = 500000.0
F32 = jnp.float32
BF16 = jnp.bfloat16

VMEM = pl.BlockSpec(memory_space=pltpu.VMEM)


def params(mib=48):
    return pltpu.CompilerParams(vmem_limit_bytes=mib * 2**20)


def dot(a, b, dims):
    return lax.dot_general(a, b, (dims, ((), ())), preferred_element_type=F32)


def iota(shape, axis):
    return lax.broadcasted_iota(jnp.int32, shape, axis)


def norm_kernel(groups, hidden_ref, gain_ref, owner_ref, owner_row_ref, completion_ref, grad_ref, *outs):
    part_refs, slot_grad_ref = outs[:-1], outs[-1]
    count, width = hidden_ref.shape
    wide = hidden_ref[...].astype(F32)
    inverse = lax.rsqrt(jnp.mean(wide * wide, axis=1, keepdims=True) + EPSILON)
    normed = (wide * inverse * gain_ref[...]).astype(BF16)
    owner = owner_ref[...]
    owner_row = owner_row_ref[...]
    same = owner == owner_row
    rows, cols = iota((count, count), 0), iota((count, count), 1)
    rank = jnp.sum(jnp.where(same & (cols < rows), 1.0, 0.0), axis=1, keepdims=True)
    rank_row = jnp.sum(jnp.where(same & (rows < cols), 1.0, 0.0), axis=0, keepdims=True)
    here = lax.axis_index("tensor").astype(F32)
    slot = owner.astype(F32) * 16.0 + here * 2.0 + rank
    lane = iota((count, EXT), 1)
    ext = jnp.where(lane == 0, slot, jnp.where(lane == 1, completion_ref[...].astype(F32) + 1.0, 0.0))
    span = width // PARTS
    for i, ref in enumerate(part_refs):
        ref[:, 0:span] = normed[:, i * span : (i + 1) * span]
    part_refs[0][:, span : span + EXT] = ext.astype(BF16)
    place = owner_row.astype(F32) * 2.0 + rank_row
    pick = (iota((2 * groups, count), 0).astype(F32) == place).astype(BF16)
    slot_grad_ref[...] = dot(pick, grad_ref[...], ((1,), (0,))).astype(BF16)


def project_kernel(count, first, last, *refs):
    refs = list(refs)
    blocks = [refs.pop(0) for _ in range(count)]
    exts = [refs.pop(0) for _ in range(count)] if last else None
    wq_ref, wk_ref, wv_ref = refs.pop(0), refs.pop(0), refs.pop(0)
    before_ref = None if first else refs.pop(0)
    out_ref = refs.pop(0)
    total = refs.pop(0) if last else out_ref
    step = pl.program_id(0)
    x = jnp.concatenate([b[...] for b in blocks], axis=0)
    qc = wq_ref.shape[1]

    def add(cols, value):
        @pl.when(step == 0)
        def _():
            total[:, cols] = value if first else before_ref[:, cols] + value

        @pl.when(step > 0)
        def _():
            total[:, cols] += value

    add(slice(0, qc), dot(x, wq_ref[...], ((1,), (0,))))
    wkv = jnp.concatenate([wk_ref[...], wv_ref[...]], axis=1)
    add(slice(qc, qc + 2 * HD), dot(x, wkv, ((1,), (0,))))

    if last:

        @pl.when(step == pl.num_programs(0) - 1)
        def _():
            ext = jnp.concatenate([e[...] for e in exts], axis=0)
            rows = ext.shape[0]
            slots = out_ref.shape[0]
            hot = (ext[:, 0:1].astype(F32) == iota((rows, slots), 1).astype(F32)).astype(BF16)
            cols = total.shape[1]
            out_ref[:, 0:cols] = dot(hot, total[...].astype(BF16), ((0,), (0,))).astype(BF16)
            out_ref[:, cols : cols + EXT] = dot(hot, ext, ((0,), (0,))).astype(BF16)


def project(blocks, exts, wq, wk, wv, part, before, last, slots):
    rows = sum(b.shape[0] for b in blocks)
    span = wq.shape[0] // PARTS
    steps = span // STEP
    cols = wq.shape[1] + wk.shape[1] + wv.shape[1]
    ext_at = span // EXT
    specs = [pl.BlockSpec((b.shape[0], STEP), lambda k: (0, k)) for b in blocks]
    operands = list(blocks)
    if last:
        specs += [pl.BlockSpec((b.shape[0], EXT), lambda k: (0, ext_at)) for b in exts]
        operands += list(exts)
    for w in (wq, wk, wv):
        specs.append(pl.BlockSpec((STEP, w.shape[1]), lambda k: (k + part * steps, 0)))
        operands.append(w)
    if before is not None:
        specs.append(pl.BlockSpec((rows, cols), lambda k: (0, 0)))
        operands.append(before)
    if last:
        out = jax.ShapeDtypeStruct((slots, cols + EXT), BF16)
        out_spec = pl.BlockSpec((slots, cols + EXT), lambda k: (0, 0))
        scratch = [pltpu.VMEM((rows, cols), F32)]
    else:
        out = jax.ShapeDtypeStruct((rows, cols), F32)
        out_spec = pl.BlockSpec((rows, cols), lambda k: (0, 0))
        scratch = []

    def body(*refs):
        project_kernel(len(blocks), before is None, last, *refs)

    return pl.pallas_call(
        body,
        grid=(steps,),
        in_specs=specs,
        out_specs=out_spec,
        out_shape=out,
        scratch_shapes=scratch,
        compiler_params=params(),
        cost_estimate=pl.CostEstimate(
            flops=2 * rows * span * cols, bytes_accessed=2 * span * cols, transcendentals=0
        ),
        name="project",
    )(*operands)


def attend_kernel(ranks, got_ref, grad_ref, rewards_ref, out_ref):
    slots = got_ref.shape[0]
    heads = grad_ref.shape[1] // HD
    kcol = heads * HD
    vcol = kcol + HD
    ecol = vcol + HD
    factor = HD**-0.5
    ext = got_ref[:, ecol : ecol + EXT].astype(F32)
    label = ext[:, 1:2]
    label_row = jnp.transpose(ext)[1:2, :]
    rows, cols = iota((slots, slots), 0), iota((slots, slots), 1)
    same = label == label_row
    allowed = same & (cols <= rows)
    position = jnp.sum(jnp.where(same & (cols < rows), 1.0, 0.0), axis=1, keepdims=True)
    lane = iota((slots, HD), 1)
    half = HD // 2
    index = jnp.where(lane < half, lane, lane - half).astype(F32)
    freq = jnp.exp(index * (-2.0 / HD * jnp.log(F32(BASE))))
    angle = position * freq
    cosine = jnp.cos(angle)
    sine = jnp.where(lane < half, -jnp.sin(angle), jnp.sin(angle))

    def rope(u, sign):
        return u * cosine + pltpu.roll(u, half, 1) * (sine * sign)

    scaled = rewards_ref[...].astype(F32) / 256.0
    advantage = scaled - (jnp.sum(scaled) - scaled) / (KC - 1)
    advantage = jnp.concatenate([advantage, jnp.zeros((1, EXT - KC), F32)], axis=1)
    weight = jnp.sum(jnp.where(label - 1.0 == lane.astype(F32), advantage, 0.0), axis=1, keepdims=True)

    dp_ranks = slots // (2 * ranks)
    source = ((rows // 2) % ranks) * (2 * dp_ranks) + (rows // (2 * ranks)) * 2 + rows % 2
    move = (cols == source).astype(BF16)
    grads = dot(move, grad_ref[...], ((1,), (0,)))
    grads = (grads * weight).astype(BF16)

    key = rope(got_ref[:, kcol : kcol + HD].astype(F32), 1.0).astype(BF16)
    value = got_ref[:, vcol : vcol + HD]
    grad_key = jnp.zeros((slots, HD), F32)
    grad_value = jnp.zeros((slots, HD), F32)
    for h in range(heads):
        at = slice(h * HD, (h + 1) * HD)
        query = rope(got_ref[:, at].astype(F32), 1.0).astype(BF16)
        grad = grads[:, at]
        scores = dot(query, key, ((1,), (1,))) * factor
        scores = jnp.where(allowed, scores, -1e30)
        highest = jnp.max(scores, axis=1, keepdims=True)
        weights = jnp.exp(scores - highest)
        probs = weights / jnp.sum(weights, axis=1, keepdims=True)
        grad_value = grad_value + dot(probs.astype(BF16), grad, ((0,), (0,)))
        grad_probs = dot(grad, value, ((1,), (1,)))
        inner = jnp.sum(probs * grad_probs, axis=1, keepdims=True)
        grad_scores = (probs * (grad_probs - inner) * factor).astype(BF16)
        grad_query = dot(grad_scores, key, ((1,), (0,)))
        grad_key = grad_key + dot(grad_scores, query, ((0,), (0,)))
        out_ref[:, at] = rope(grad_query, -1.0).astype(BF16)
    out_ref[:, kcol : kcol + HD] = rope(grad_key, -1.0).astype(BF16)
    out_ref[:, vcol : vcol + HD] = grad_value.astype(BF16)


def back_kernel(count, *refs):
    exts = refs[:count]
    slots_ref, wq_ref, wk_ref, wv_ref, keep_ref, send_ref, held = refs[count:]
    half = keep_ref.shape[0]
    qc = wq_ref.shape[1]

    @pl.when(pl.program_id(0) == 0)
    def _():
        ext = jnp.concatenate([e[...] for e in exts], axis=0)
        slots = slots_ref.shape[0]
        hot = (ext[:, 0:1].astype(F32) == iota((ext.shape[0], slots), 1).astype(F32)).astype(BF16)
        held[...] = dot(hot, slots_ref[...], ((1,), (0,))).astype(BF16)

    wkv = jnp.concatenate([wk_ref[...], wv_ref[...]], axis=1)
    term = dot(held[:, 0:qc], wq_ref[...], ((1,), (1,))) + dot(held[:, qc:], wkv, ((1,), (1,)))
    term = term.astype(BF16)
    keep_ref[...] = term[0:half]
    send_ref[...] = term[half:]


def back(exts, slot_grads, wq, wk, wv, part):
    rows = sum(e.shape[0] for e in exts)
    span = wq.shape[0] // PARTS
    steps = span // STEP
    ext_at = span // EXT
    cols = wq.shape[1] + wk.shape[1] + wv.shape[1]
    specs = [pl.BlockSpec((e.shape[0], EXT), lambda k: (0, ext_at)) for e in exts]
    specs.append(pl.BlockSpec(slot_grads.shape, lambda k: (0, 0)))
    for w in (wq, wk, wv):
        specs.append(pl.BlockSpec((STEP, w.shape[1]), lambda k: (k + part * steps, 0)))

    def body(*refs):
        back_kernel(len(exts), *refs)

    out = jax.ShapeDtypeStruct((rows // 2, span), BF16)
    out_spec = pl.BlockSpec((rows // 2, STEP), lambda k: (0, k))
    return pl.pallas_call(
        body,
        grid=(steps,),
        in_specs=specs,
        out_specs=[out_spec, out_spec],
        out_shape=[out, out],
        scratch_shapes=[pltpu.VMEM((rows, cols), BF16)],
        compiler_params=params(),
        cost_estimate=pl.CostEstimate(
            flops=2 * rows * span * cols, bytes_accessed=2 * span * cols, transcendentals=0
        ),
        name="back",
    )(*exts, slot_grads, wq, wk, wv)


def finish_kernel(hidden_ref, gain_ref, *refs):
    out_ref = refs[-1]
    wide = hidden_ref[...].astype(F32)
    inverse = lax.rsqrt(jnp.mean(wide * wide, axis=1, keepdims=True) + EPSILON)
    parts = []
    for i in range(PARTS):
        a, b, c = refs[3 * i : 3 * i + 3]
        parts.append(a[...].astype(F32) + b[...].astype(F32) + c[...].astype(F32))
    scaled = jnp.concatenate(parts, axis=1) * gain_ref[...]
    inner = jnp.mean(scaled * wide, axis=1, keepdims=True)
    out_ref[...] = (inverse * scaled - wide * inverse * inverse * inverse * inner).astype(BF16)


def on_device(hidden, gain, w_query, w_key, w_value, out_grad, owner, completion, rewards):
    groups = lax.axis_size("dp")
    ranks = lax.axis_size("tensor")
    chips = ranks // 2
    count, width = hidden.shape
    query_cols = w_query.shape[1]
    slots = 2 * groups * ranks
    span = width // PARTS

    swap_pairs = [(t, t ^ 1) for t in range(ranks)]
    flow_pairs = [(t, (t // 2 + (1 if t % 2 == 0 else chips - 1)) % chips * 2 + t % 2) for t in range(ranks)]

    def swap(x):
        return lax.ppermute(x, "tensor", swap_pairs)

    def flow(x):
        return lax.ppermute(x, "tensor", flow_pairs)

    row_types = [jax.ShapeDtypeStruct((count, span + (EXT if i == 0 else 0)), BF16) for i in range(PARTS)]
    *mine, slot_grad = pl.pallas_call(
        lambda *refs: norm_kernel(groups, *refs),
        in_specs=[VMEM] * 6,
        out_specs=[VMEM] * (PARTS + 1),
        out_shape=row_types + [jax.ShapeDtypeStruct((2 * groups, width), BF16)],
        compiler_params=params(),
        name="norm",
    )(hidden, gain.reshape(1, width), owner, owner.reshape(1, count), completion.reshape(count, 1), out_grad)

    by_group = lax.all_to_all(slot_grad.reshape(groups, 2, width), "dp", split_axis=0, concat_axis=0, tiled=True)
    by_group = by_group.reshape(2 * groups, ranks, query_cols).transpose(1, 0, 2)
    by_head = lax.all_to_all(by_group, "tensor", split_axis=0, concat_axis=0, tiled=True)
    grad_slots = by_head.reshape(slots, query_cols)

    blocks = []
    total = None
    for i in range(PARTS):
        m = mine[i]
        ms = swap(m)
        near = flow(jnp.concatenate([m, ms], axis=0))
        far = flow(near[:count])
        nears = swap(near)
        fars = swap(far)
        blocks.append((m, ms, near, nears, far, fars))
    exts = blocks[0]
    for i in range(PARTS):
        last = i == PARTS - 1
        total = project(blocks[i], exts if last else None, w_query, w_key, w_value, i, total, last, slots)
    got = lax.all_to_all(
        total.reshape(groups, 2 * ranks, total.shape[1]), "dp", split_axis=0, concat_axis=0, tiled=True
    ).reshape(total.shape)

    grads = pl.pallas_call(
        lambda *refs: attend_kernel(ranks, *refs),
        in_specs=[VMEM] * 3,
        out_specs=VMEM,
        out_shape=jax.ShapeDtypeStruct((slots, total.shape[1] - EXT), BF16),
        compiler_params=params(),
        name="attend",
    )(got, grad_slots, rewards)
    slot_grads = lax.all_to_all(
        grads.reshape(groups, 2 * ranks, grads.shape[1]), "dp", split_axis=0, concat_axis=0, tiled=True
    ).reshape(grads.shape)

    m, ms, near, nears, far, fars = exts
    pieces = []
    for i in range(PARTS):
        keep, send = back((m, nears, far, ms, near, fars), slot_grads, w_query, w_key, w_value, i)
        both = (keep.astype(F32) + swap(send).astype(F32)).astype(BF16)
        passed = flow(both[3 * count :])
        onward = both[count : 3 * count]
        onward = jnp.concatenate(
            [onward[:count], (onward[count:].astype(F32) + passed.astype(F32)).astype(BF16)], axis=0
        )
        came = flow(onward)
        pieces += [both[:count], came[count:], swap(came[:count])]

    return pl.pallas_call(
        finish_kernel,
        in_specs=[VMEM] * (2 + len(pieces)),
        out_specs=VMEM,
        out_shape=jax.ShapeDtypeStruct((count, width), BF16),
        compiler_params=params(),
        name="finish",
    )(hidden, gain.reshape(1, width), *pieces)


def solution(mesh):
    return jax.shard_map(
        on_device,
        mesh=mesh,
        in_specs=(
            P(("dp", "tensor"), None),
            P(),
            P(None, "tensor"),
            P(None, "tensor"),
            P(None, "tensor"),
            P(("dp", "tensor"), None),
            P(("dp", "tensor"), None),
            P(("dp", "tensor")),
            P("dp", None),
        ),
        out_specs=P(("dp", "tensor"), None),
        check_vma=False,
    )
```

```python
import jax
import jax.numpy as jnp
from jax import lax
from jax.experimental import pallas as pl
from jax.experimental.pallas import tpu as pltpu
from jax.sharding import PartitionSpec as P

HD = 128
KC = 16
PARTS = 2
EXT = 128
STEP = 1024
PIECES = 4
EPSILON = 1e-05
BASE = 500000.0
F32 = jnp.float32
BF16 = jnp.bfloat16

VMEM = pl.BlockSpec(memory_space=pltpu.VMEM)
ANY = pl.BlockSpec(memory_space=pl.ANY)


def params(mib=12):
    return pltpu.CompilerParams(vmem_limit_bytes=mib * 2**20)


def in_hbm(x):
    return pltpu.with_memory_space_constraint(x, pltpu.HBM)


def dot(a, b, dims):
    return lax.dot_general(a, b, (dims, ((), ())), preferred_element_type=F32)


def iota(shape, axis):
    return lax.broadcasted_iota(jnp.int32, shape, axis)


def norm_kernel(hidden_hbm, gain_hbm, owner_hbm, completion_hbm, out_ref, *rest):
    hidden_ref, gain_ref, owner_ref, completion_ref, sems = rest
    copies = [
        pltpu.make_async_copy(src, dst, sems.at[i])
        for i, (src, dst) in enumerate(
            (
                (hidden_hbm, hidden_ref),
                (gain_hbm, gain_ref),
                (owner_hbm, owner_ref),
                (completion_hbm, completion_ref),
            )
        )
    ]
    for copy in copies:
        copy.start()
    for copy in copies:
        copy.wait()
    count, width = hidden_ref.shape
    wide = hidden_ref[...].astype(F32)
    inverse = lax.rsqrt(jnp.mean(wide * wide, axis=1, keepdims=True) + EPSILON)
    rows, cols = iota((count, count), 0), iota((count, count), 1)
    owner_row = owner_ref[...].astype(F32)
    owner = jnp.sum(jnp.where(rows == cols, owner_row, 0.0), axis=1, keepdims=True)
    label = jnp.sum(
        jnp.where(rows == cols, completion_ref[...].astype(F32) + 1.0, 0.0), axis=1, keepdims=True
    )
    rank = jnp.sum(jnp.where((owner == owner_row) & (cols < rows), 1.0, 0.0), axis=1, keepdims=True)
    here = lax.axis_index("tensor").astype(F32)
    slot = owner * 16.0 + here * 2.0 + rank
    lane = iota((count, EXT), 1)
    ext = jnp.where(lane == 0, slot, jnp.where(lane == 1, label, 0.0))
    out_ref[:, 0:width] = (wide * inverse * gain_ref[...]).astype(BF16)
    out_ref[:, width:] = ext.astype(BF16)


def join_kernel(mine_ref, other_ref, *part_refs):
    count = mine_ref.shape[0]
    at = 0
    for ref in part_refs:
        n = ref.shape[1]
        ref[0:count, :] = mine_ref[:, at : at + n]
        ref[count:, :] = other_ref[:, at : at + n]
        at += n


def pack_kernel(grad_ref, mine_ref, _, out_ref):
    count = grad_ref.shape[0]
    n = out_ref.shape[1] - EXT
    for t in range(grad_ref.shape[1] // n):
        at = slice(t * count, (t + 1) * count)
        out_ref[at, 0:n] = grad_ref[:, t * n : (t + 1) * n]
        out_ref[at, n:] = mine_ref[:, mine_ref.shape[1] - EXT :]


def relay_kernel(near_ref, out_ref):
    out_ref[...] = near_ref[0 : out_ref.shape[0], :]


def gather_rows(blocks, x_ref):
    at = 0
    span = x_ref.shape[1]
    for b in blocks:
        x_ref[at : at + b.shape[0], :] = b[:, 0:span]
        at += b.shape[0]


def weight_copies(part, weights, w_ref, sems):
    span = w_ref.shape[0]
    step = span // PIECES
    copies = []
    for j in range(PIECES):
        at = 0
        for w in weights:
            n = w.shape[1]
            copies.append(
                pltpu.make_async_copy(
                    w.at[pl.ds(part * span + j * step, step), :],
                    w_ref.at[pl.ds(j * step, step), pl.ds(at, n)],
                    sems.at[len(copies)],
                )
            )
            at += n
    return copies


def project_kernel(part, count, last, *refs):
    blocks = refs[:count]
    weights = refs[count : count + 3]
    rest = refs[count + 3 :]
    x_ref, w_ref, total_ref, sems = rest[-4:]
    span = x_ref.shape[1]
    step = span // PIECES
    copies = weight_copies(part, weights, w_ref, sems)
    for copy in copies:
        copy.start()
    gather_rows(blocks, x_ref)
    for j in range(PIECES):
        for copy in copies[3 * j : 3 * j + 3]:
            copy.wait()
        at = slice(j * step, (j + 1) * step)
        value = dot(x_ref[:, at], w_ref[at, :], ((1,), (0,)))
        if j > 0:
            value += total_ref[...]
        elif last:
            value += rest[0][...]
        total_ref[...] = value
    if not last:
        return
    _, grad_ref, out_ref, ext_ref = rest[:4]
    total = total_ref[...].astype(BF16)
    cols = total.shape[1]
    slots = out_ref.shape[0]
    both, near, nears, far, fars = [e[:, span : span + EXT] for e in blocks]
    ext = jnp.concatenate([both, near, nears, far, fars], axis=0)

    def hot(ext):
        return (ext[:, 0:1].astype(F32) == iota((ext.shape[0], slots), 1).astype(F32)).astype(BF16)

    spread = hot(ext)
    out_ref[:, 0:cols] = dot(spread, total, ((0,), (0,))).astype(BF16)
    out_ref[:, cols : cols + EXT] = dot(spread, ext, ((0,), (0,))).astype(BF16)
    n = grad_ref.shape[1] - EXT
    out_ref[:, cols + EXT :] = dot(hot(grad_ref[:, n:]), grad_ref[:, 0:n], ((0,), (0,))).astype(BF16)
    half = both.shape[0] // 2
    ext_ref[...] = jnp.concatenate([both[:half], nears, far, both[half:], near, fars], axis=0)


def project(part, blocks, weights, before, grads, slots):
    rows = sum(b.shape[0] for b in blocks)
    width = weights[0].shape[0]
    span = width // PARTS
    cols = sum(w.shape[1] for w in weights)
    last = before is not None
    sums = jax.ShapeDtypeStruct((rows, cols), F32)
    out = sums
    if last:
        out = [
            jax.ShapeDtypeStruct((slots, cols + grads.shape[1]), BF16),
            jax.ShapeDtypeStruct((rows, EXT), BF16),
        ]
    scratch = [pltpu.VMEM((rows, span), BF16), pltpu.VMEM((span, cols), BF16)]
    if last:
        scratch.append(pltpu.VMEM((rows, cols), F32))
    scratch.append(pltpu.SemaphoreType.DMA((3 * PIECES,)))

    def body(*refs):
        refs = list(refs)
        if not last:
            sums_ref = refs.pop(len(blocks) + 3)
            refs.insert(len(refs) - 1, sums_ref)
        project_kernel(part, len(blocks), last, *refs)

    return pl.pallas_call(
        body,
        in_specs=[VMEM] * len(blocks) + [ANY] * 3 + ([VMEM] * 2 if last else []),
        out_specs=[VMEM] * 2 if last else VMEM,
        out_shape=out,
        scratch_shapes=scratch,
        compiler_params=params(20),
        cost_estimate=pl.CostEstimate(
            flops=2 * rows * span * cols, bytes_accessed=2 * span * cols, transcendentals=0
        ),
        name="project",
    )(*blocks, *[in_hbm(w) for w in weights], *([before, grads] if last else []))


def attend_kernel(got_ref, rewards_ref, out_ref):
    slots = got_ref.shape[0]
    heads = out_ref.shape[1] // HD - 2
    kcol = heads * HD
    vcol = kcol + HD
    ecol = vcol + HD
    gcol = ecol + EXT
    factor = HD**-0.5
    ext = got_ref[:, ecol : ecol + EXT].astype(F32)
    label = ext[:, 1:2]
    label_row = jnp.transpose(ext)[1:2, :]
    rows, cols = iota((slots, slots), 0), iota((slots, slots), 1)
    same = label == label_row
    bias = jnp.where(same & (rows <= cols), 0.0, -1e30)
    position = jnp.sum(jnp.where(same & (cols < rows), 1.0, 0.0), axis=1, keepdims=True)
    lane = iota((slots, HD), 1)
    half = HD // 2
    index = jnp.where(lane < half, lane, lane - half).astype(F32)
    freq = jnp.exp(index * (-2.0 / HD * jnp.log(F32(BASE))))
    angle = position * freq
    cosine = jnp.cos(angle)
    sine = jnp.sin(angle)
    sine = jnp.where(lane < half, -sine, sine)

    def rope(u):
        return u * cosine + pltpu.roll(u, half, 1) * sine

    def rope_back(u):
        return u * cosine - pltpu.roll(u, half, 1) * sine

    scaled = rewards_ref[...].astype(F32) / 256.0
    advantage = scaled - (jnp.sum(scaled) - scaled) / (KC - 1)
    advantage = jnp.concatenate([advantage, jnp.zeros((1, EXT - KC), F32)], axis=1)
    weight = jnp.sum(jnp.where(label - 1.0 == lane.astype(F32), advantage, 0.0), axis=1, keepdims=True)

    key = rope(got_ref[:, kcol : kcol + HD].astype(F32)).astype(BF16)
    value = got_ref[:, vcol : vcol + HD]
    grad_key = jnp.zeros((slots, HD), F32)
    grad_value = jnp.zeros((slots, HD), F32)
    for h in range(heads):
        at = slice(h * HD, (h + 1) * HD)
        query = rope(got_ref[:, at].astype(F32)).astype(BF16)
        grad = (got_ref[:, gcol + h * HD : gcol + (h + 1) * HD].astype(F32) * weight).astype(BF16)
        scores = dot(key, query, ((1,), (1,))) * factor + bias
        highest = jnp.max(scores, axis=0, keepdims=True)
        weights = jnp.exp(scores - highest)
        probs = weights * (1.0 / jnp.sum(weights, axis=0, keepdims=True))
        grad_value = grad_value + dot(probs.astype(BF16), grad, ((1,), (0,)))
        grad_probs = dot(value, grad, ((1,), (1,)))
        inner = jnp.sum(probs * grad_probs, axis=0, keepdims=True)
        grad_scores = (probs * (grad_probs - inner) * factor).astype(BF16)
        grad_query = dot(grad_scores, key, ((0,), (0,)))
        grad_key = grad_key + dot(grad_scores, query, ((1,), (0,)))
        out_ref[:, at] = rope_back(grad_query).astype(BF16)
    out_ref[:, kcol : kcol + HD] = rope_back(grad_key).astype(BF16)
    out_ref[:, vcol : vcol + HD] = grad_value.astype(BF16)


def back_kernel(part, ext_ref, slots_ref, wq_hbm, wk_hbm, wv_hbm, keep_ref, send_ref, w_ref, sems):
    span = w_ref.shape[0]
    step = span // PIECES
    copies = weight_copies(part, (wq_hbm, wk_hbm, wv_hbm), w_ref, sems)
    for copy in copies:
        copy.start()
    half = keep_ref.shape[0]
    slots = slots_ref.shape[0]
    hot = (ext_ref[:, 0:1].astype(F32) == iota((ext_ref.shape[0], slots), 1).astype(F32)).astype(BF16)
    held = dot(hot, slots_ref[...], ((1,), (0,))).astype(BF16)
    for j in range(PIECES):
        for copy in copies[3 * j : 3 * j + 3]:
            copy.wait()
        at = slice(j * step, (j + 1) * step)
        term = dot(held, w_ref[at, :], ((1,), (1,))).astype(BF16)
        keep_ref[:, at] = term[0:half]
        send_ref[:, at] = term[half:]


def back(part, ext, slot_grads, weights):
    rows = ext.shape[0]
    width = weights[0].shape[0]
    span = width // PARTS
    cols = sum(w.shape[1] for w in weights)
    out = jax.ShapeDtypeStruct((rows // 2, span), BF16)
    return pl.pallas_call(
        lambda *refs: back_kernel(part, *refs),
        in_specs=[VMEM, VMEM] + [ANY] * 3,
        out_specs=[VMEM] * 2,
        out_shape=[out, out],
        scratch_shapes=[pltpu.VMEM((span, cols), BF16), pltpu.SemaphoreType.DMA((3 * PIECES,))],
        compiler_params=params(20),
        cost_estimate=pl.CostEstimate(
            flops=2 * rows * span * cols, bytes_accessed=2 * span * cols, transcendentals=0
        ),
        name="back",
    )(ext, slot_grads, *[in_hbm(w) for w in weights])


def finish_kernel(hidden_ref, gain_ref, *refs):
    out_ref = refs[-1]
    wide = hidden_ref[...].astype(F32)
    inverse = lax.rsqrt(jnp.mean(wide * wide, axis=1, keepdims=True) + EPSILON)
    parts = []
    for i in range(PARTS):
        a, b, c = refs[3 * i : 3 * i + 3]
        parts.append(a[...].astype(F32) + b[...].astype(F32) + c[...].astype(F32))
    scaled = jnp.concatenate(parts, axis=1) * gain_ref[...]
    inner = jnp.mean(scaled * wide, axis=1, keepdims=True)
    out_ref[...] = (inverse * scaled - wide * inverse * inverse * inverse * inner).astype(BF16)


def on_device(hidden, gain, w_query, w_key, w_value, out_grad, owner, completion, rewards):
    groups = lax.axis_size("dp")
    ranks = lax.axis_size("tensor")
    chips = ranks // 2
    count, width = hidden.shape
    query_cols = w_query.shape[1]
    slots = 2 * groups * ranks
    span = width // PARTS

    swap_pairs = [(t, t ^ 1) for t in range(ranks)]
    flow_pairs = [(t, (t // 2 + (1 if t % 2 == 0 else chips - 1)) % chips * 2 + t % 2) for t in range(ranks)]

    def swap(x):
        return lax.ppermute(x, "tensor", swap_pairs)

    def flow(x):
        return lax.ppermute(x, "tensor", flow_pairs)

    mine = pl.pallas_call(
        norm_kernel,
        in_specs=[ANY] * 4,
        out_specs=VMEM,
        out_shape=jax.ShapeDtypeStruct((count, width + EXT), BF16),
        scratch_shapes=[
            pltpu.VMEM((count, width), BF16),
            pltpu.VMEM((1, width), F32),
            pltpu.VMEM((1, count), jnp.int32),
            pltpu.VMEM((1, count), jnp.int32),
            pltpu.SemaphoreType.DMA((4,)),
        ],
        compiler_params=params(),
        name="norm",
    )(*[in_hbm(x) for x in (hidden, gain.reshape(1, width), owner.reshape(1, count), completion.reshape(1, count))])
    other = swap(mine)
    sent = pl.pallas_call(
        join_kernel,
        in_specs=[VMEM] * 2,
        out_specs=[VMEM] * PARTS,
        out_shape=[
            jax.ShapeDtypeStruct((2 * count, span + (EXT if i == PARTS - 1 else 0)), BF16)
            for i in range(PARTS)
        ],
        compiler_params=params(),
        name="join",
    )(mine, other)

    weights = (w_query, w_key, w_value)
    blocks = []
    for i in range(PARTS):
        near = flow(sent[i])
        passed = pl.pallas_call(
            relay_kernel,
            in_specs=[VMEM],
            out_specs=VMEM,
            out_shape=jax.ShapeDtypeStruct((count, near.shape[1]), BF16),
            compiler_params=params(),
            name="relay",
        )(near)
        far = flow(passed)
        blocks.append((sent[i], near, swap(near), far, swap(far)))

    by_head = pl.pallas_call(
        pack_kernel,
        in_specs=[VMEM, VMEM, ANY],
        out_specs=VMEM,
        out_shape=jax.ShapeDtypeStruct((ranks * count, query_cols + EXT), BF16),
        compiler_params=params(),
        name="pack",
    )(out_grad, mine, blocks[PARTS - 1][1])
    head_rows = lax.all_to_all(by_head, "tensor", split_axis=0, concat_axis=0, tiled=True)

    before = None
    for i in range(PARTS):
        before = project(i, blocks[i], weights, before, head_rows, slots)
    total, ext = before
    got = lax.all_to_all(
        total.reshape(groups, 2 * ranks, total.shape[1]), "dp", split_axis=0, concat_axis=0, tiled=True
    ).reshape(total.shape)

    cols = sum(w.shape[1] for w in weights)
    grads = pl.pallas_call(
        attend_kernel,
        in_specs=[VMEM] * 2,
        out_specs=VMEM,
        out_shape=jax.ShapeDtypeStruct((slots, cols), BF16),
        compiler_params=params(),
        name="attend",
    )(got, rewards)
    slot_grads = lax.all_to_all(
        grads.reshape(groups, 2 * ranks, cols), "dp", split_axis=0, concat_axis=0, tiled=True
    ).reshape(grads.shape)

    pieces = []
    for i in range(PARTS):
        keep, send = back(i, ext, slot_grads, weights)
        both = (keep.astype(F32) + swap(send).astype(F32)).astype(BF16)
        passed = flow(both[3 * count :])
        onward = both[count : 3 * count]
        onward = jnp.concatenate(
            [onward[:count], (onward[count:].astype(F32) + passed.astype(F32)).astype(BF16)], axis=0
        )
        came = flow(onward)
        pieces += [both[:count], came[count:], swap(came[:count])]

    return pl.pallas_call(
        finish_kernel,
        in_specs=[VMEM] * (2 + len(pieces)),
        out_specs=VMEM,
        out_shape=jax.ShapeDtypeStruct((count, width), BF16),
        compiler_params=params(),
        name="finish",
    )(hidden, gain.reshape(1, width), *pieces)


def solution(mesh):
    return jax.shard_map(
        on_device,
        mesh=mesh,
        in_specs=(
            P(("dp", "tensor"), None),
            P(),
            P(None, "tensor"),
            P(None, "tensor"),
            P(None, "tensor"),
            P(("dp", "tensor"), None),
            P(("dp", "tensor"), None),
            P(("dp", "tensor")),
            P("dp", None),
        ),
        out_specs=P(("dp", "tensor"), None),
        check_vma=False,
    )
```

```python
import jax
import jax.numpy as jnp
from jax import lax
from jax.experimental import pallas as pl
from jax.experimental.pallas import tpu as pltpu
from jax.sharding import PartitionSpec as P

HD = 128
KC = 16
PARTS = 2
EXT = 128
HEADS_AT = 8192 + EXT
STEP = 1024
PIECES = 4
EPSILON = 1e-05
BASE = 500000.0
F32 = jnp.float32
BF16 = jnp.bfloat16

TOKEN = jax.ShapeDtypeStruct((8, 128), F32)
VMEM = pl.BlockSpec(memory_space=pltpu.VMEM)
ANY = pl.BlockSpec(memory_space=pl.ANY)


def params(mib=12):
    return pltpu.CompilerParams(vmem_limit_bytes=mib * 2**20)


def in_hbm(x):
    return pltpu.with_memory_space_constraint(x, pltpu.HBM)


def in_vmem(x):
    return pltpu.with_memory_space_constraint(x, pltpu.VMEM)


def dot(a, b, dims):
    return lax.dot_general(a, b, (dims, ((), ())), preferred_element_type=F32)


def iota(shape, axis):
    return lax.broadcasted_iota(jnp.int32, shape, axis)


def chip_and_core():
    here = lax.axis_index("tensor")
    return here // 2, here % 2, lax.axis_size("tensor") // 2


def norm_kernel(hidden_hbm, gain_hbm, owner_hbm, completion_hbm, grad_hbm, leave_ref, cross_ref, own_ref, *rest):
    hidden_ref, gain_ref, owner_ref, completion_ref, grad_ref, sems = rest
    copies = [
        pltpu.make_async_copy(src, dst, sems.at[i])
        for i, (src, dst) in enumerate(
            (
                (hidden_hbm, hidden_ref),
                (gain_hbm, gain_ref),
                (owner_hbm, owner_ref),
                (completion_hbm, completion_ref),
                (grad_hbm, grad_ref),
            )
        )
    ]
    for copy in copies:
        copy.start()
    for copy in copies:
        copy.wait()
    count, width = hidden_ref.shape
    wide = hidden_ref[...].astype(F32)
    inverse = lax.rsqrt(jnp.mean(wide * wide, axis=1, keepdims=True) + EPSILON)
    rows, cols = iota((count, count), 0), iota((count, count), 1)
    owner_row = owner_ref[...].astype(F32)
    owner = jnp.sum(jnp.where(rows == cols, owner_row, 0.0), axis=1, keepdims=True)
    label = jnp.sum(
        jnp.where(rows == cols, completion_ref[...].astype(F32) + 1.0, 0.0), axis=1, keepdims=True
    )
    rank = jnp.sum(jnp.where((owner == owner_row) & (cols < rows), 1.0, 0.0), axis=1, keepdims=True)
    here = lax.axis_index("tensor").astype(F32)
    slot = owner * 16.0 + here * 2.0 + rank
    lane = iota((count, EXT), 1)
    ext = jnp.where(lane == 0, slot, jnp.where(lane == 1, label, 0.0)).astype(BF16)
    normed = (wide * inverse * gain_ref[...]).astype(BF16)
    for ref in (leave_ref, cross_ref):
        ref[:, 0:width] = normed
        ref[:, width : width + EXT] = ext
    chip, core, chips = chip_and_core()
    each = own_ref.shape[1]

    def heads(at, n):
        return grad_ref[:, pl.ds(pl.multiple_of(at * each, each), n * each)]

    up, down = (chip + 1) % chips, (chip + chips - 1) % chips
    at = width + EXT
    leave_ref[:, at : at + 2 * each] = heads(2 * jnp.where(core == 0, up, down), 2)
    leave_ref[:, at + 2 * each :] = heads(2 * ((chip + 2) % chips), 2)
    cross_ref[:, at : at + 2 * each] = heads(2 * jnp.where(core == 0, down, up), 2)
    cross_ref[:, at + 2 * each :] = heads(2 * chip + 1 - core, 1)
    own_ref[...] = heads(2 * chip + core, 1)


def join_kernel(mine_ref, other_ref, mine_out, other_out):
    mine_out[...] = mine_ref[...]
    other_out[...] = other_ref[:, 0 : other_out.shape[1]]


def half(rows_ref, out_ref):
    n = HEADS_AT
    each = out_ref.shape[1] - n
    _, core, _ = chip_and_core()
    out_ref[:, 0:n] = rows_ref[:, 0:n]
    first, second = rows_ref[:, n : n + each], rows_ref[:, n + each : n + 2 * each]
    out_ref[:, n:] = jnp.where(core == 0, second, first)


def half_kernel(rows_ref, _, out_ref):
    half(rows_ref, out_ref)


def relay_kernel(near_ref, _, pass_ref, half_ref):
    n = HEADS_AT
    each = half_ref.shape[1] - n
    pass_ref[:, 0:n] = near_ref[:, 0:n]
    pass_ref[:, n:] = near_ref[:, n + 2 * each :]
    half(near_ref, half_ref)


def load_kernel(part, wq_hbm, wk_hbm, wv_hbm, _, out_ref, token_ref, sems):
    token_ref[...] = jnp.zeros_like(token_ref)
    span = out_ref.shape[0]
    step = span // PIECES
    copies = []
    at = 0
    for w in (wq_hbm, wk_hbm, wv_hbm):
        n = w.shape[1]
        for j in range(PIECES):
            copies.append(
                pltpu.make_async_copy(
                    w.at[pl.ds(part * span + j * step, step), :],
                    out_ref.at[pl.ds(j * step, step), pl.ds(at, n)],
                    sems.at[len(copies)],
                )
            )
        at += n
    for copy in copies:
        copy.start()
    for copy in copies:
        copy.wait()


def load(part, weights, after):
    span = weights[0].shape[0] // PARTS
    cols = sum(w.shape[1] for w in weights)
    return pl.pallas_call(
        lambda *refs: load_kernel(part, *refs),
        in_specs=[ANY] * 3 + [VMEM],
        out_specs=[VMEM] * 2,
        out_shape=[pltpu.VMEM((span, cols), BF16), TOKEN],
        scratch_shapes=[pltpu.SemaphoreType.DMA((3 * PIECES,))],
        compiler_params=params(),
        cost_estimate=pl.CostEstimate(flops=0, bytes_accessed=2 * span * cols, transcendentals=0),
        name="load",
    )(*[in_hbm(w) for w in weights], after)


def project_kernel(count, *refs):
    blocks = refs[:count]
    parts = refs[count : count + PARTS]
    own_ref, out_ref, ext_ref, x_ref = refs[count + PARTS :]
    width = x_ref.shape[1]
    rows = blocks[0].shape[0]
    for i, b in enumerate(blocks):
        x_ref[i * rows : (i + 1) * rows, :] = b[:, 0:width]
    exts = [b[:, width : width + EXT] for b in blocks]
    mine, other, near, near_o, across, across_o, far, far_o = exts
    ext_ref[...] = jnp.concatenate([mine, across, across_o, far, other, near, near_o, far_o], axis=0)
    total = None
    for i, w in enumerate(parts):
        span = w.shape[0]
        value = dot(x_ref[:, i * span : (i + 1) * span], w[...], ((1,), (0,)))
        total = value if total is None else total + value
    total = total.astype(BF16)
    cols = total.shape[1]
    slots = out_ref.shape[0]
    ext = jnp.concatenate(exts, axis=0)
    spread = (ext[:, 0:1].astype(F32) == iota((ext.shape[0], slots), 1).astype(F32)).astype(BF16)
    out_ref[:, 0:cols] = dot(spread, total, ((0,), (0,))).astype(BF16)
    out_ref[:, cols : cols + EXT] = dot(spread, ext, ((0,), (0,))).astype(BF16)
    _, core, _ = chip_and_core()
    n = HEADS_AT
    each = own_ref.shape[1]

    def heads(b):
        return jnp.where(core == 0, b[:, n : n + each], b[:, n + each : n + 2 * each])

    mine, other, near, near_o, across, across_o, far, far_o = blocks
    grads = [own_ref[...], other[:, n + 2 * each :], heads(near), heads(near_o)]
    grads += [across[:, n:], across_o[:, n:], heads(far), far_o[:, n:]]
    out_ref[:, cols + EXT :] = dot(spread, jnp.concatenate(grads, axis=0), ((0,), (0,))).astype(BF16)


def project(blocks, loaded, own, slots):
    rows = sum(b.shape[0] for b in blocks)
    span, cols = loaded[0].shape
    width = span * PARTS
    return pl.pallas_call(
        lambda *refs: project_kernel(len(blocks), *refs),
        in_specs=[VMEM] * (len(blocks) + PARTS + 1),
        out_specs=[VMEM] * 2,
        out_shape=[
            jax.ShapeDtypeStruct((slots, cols + EXT + own.shape[1]), BF16),
            jax.ShapeDtypeStruct((rows, EXT), BF16),
        ],
        scratch_shapes=[pltpu.VMEM((rows, width), BF16)],
        compiler_params=params(),
        cost_estimate=pl.CostEstimate(
            flops=2 * rows * width * cols, bytes_accessed=2 * width * cols, transcendentals=0
        ),
        name="project",
    )(*blocks, *[in_vmem(w) for w in loaded], own)


def attend_kernel(got_ref, rewards_ref, out_ref):
    slots = got_ref.shape[0]
    heads = out_ref.shape[1] // HD - 2
    kcol = heads * HD
    vcol = kcol + HD
    ecol = vcol + HD
    gcol = ecol + EXT
    factor = HD**-0.5
    ext = got_ref[:, ecol : ecol + EXT].astype(F32)
    label = ext[:, 1:2]
    label_row = jnp.transpose(ext)[1:2, :]
    rows, cols = iota((slots, slots), 0), iota((slots, slots), 1)
    same = label == label_row
    bias = jnp.where(same & (rows <= cols), 0.0, -1e30)
    position = jnp.sum(jnp.where(same & (cols < rows), 1.0, 0.0), axis=1, keepdims=True)
    lane = iota((slots, HD), 1)
    half = HD // 2
    index = jnp.where(lane < half, lane, lane - half).astype(F32)
    freq = jnp.exp(index * (-2.0 / HD * jnp.log(F32(BASE))))
    angle = position * freq
    cosine = jnp.cos(angle)
    sine = jnp.sin(angle)
    sine = jnp.where(lane < half, -sine, sine)

    def rope(u):
        return u * cosine + pltpu.roll(u, half, 1) * sine

    def rope_back(u):
        return u * cosine - pltpu.roll(u, half, 1) * sine

    scaled = rewards_ref[...].astype(F32) / 256.0
    advantage = scaled - (jnp.sum(scaled) - scaled) / (KC - 1)
    advantage = jnp.concatenate([advantage, jnp.zeros((1, EXT - KC), F32)], axis=1)
    weight = jnp.sum(jnp.where(label - 1.0 == lane.astype(F32), advantage, 0.0), axis=1, keepdims=True)

    key = rope(got_ref[:, kcol : kcol + HD].astype(F32)).astype(BF16)
    value = got_ref[:, vcol : vcol + HD]
    grad_key = jnp.zeros((slots, HD), F32)
    grad_value = jnp.zeros((slots, HD), F32)
    for h in range(heads):
        at = slice(h * HD, (h + 1) * HD)
        query = rope(got_ref[:, at].astype(F32)).astype(BF16)
        grad = (got_ref[:, gcol + h * HD : gcol + (h + 1) * HD].astype(F32) * weight).astype(BF16)
        scores = dot(key, query, ((1,), (1,))) * factor + bias
        highest = jnp.max(scores, axis=0, keepdims=True)
        weights = jnp.exp(scores - highest)
        probs = weights * (1.0 / jnp.sum(weights, axis=0, keepdims=True))
        grad_value = grad_value + dot(probs.astype(BF16), grad, ((1,), (0,)))
        grad_probs = dot(value, grad, ((1,), (1,)))
        inner = jnp.sum(probs * grad_probs, axis=0, keepdims=True)
        grad_scores = (probs * (grad_probs - inner) * factor).astype(BF16)
        grad_query = dot(grad_scores, key, ((0,), (0,)))
        grad_key = grad_key + dot(grad_scores, query, ((1,), (0,)))
        out_ref[:, at] = rope_back(grad_query).astype(BF16)
    out_ref[:, kcol : kcol + HD] = rope_back(grad_key).astype(BF16)
    out_ref[:, vcol : vcol + HD] = grad_value.astype(BF16)


def weight_copies(part, weights, w_ref, sems):
    span = w_ref.shape[0]
    step = span // PIECES
    copies = []
    for j in range(PIECES):
        at = 0
        for w in weights:
            n = w.shape[1]
            copies.append(
                pltpu.make_async_copy(
                    w.at[pl.ds(part * span + j * step, step), :],
                    w_ref.at[pl.ds(j * step, step), pl.ds(at, n)],
                    sems.at[len(copies)],
                )
            )
            at += n
    return copies


def back_kernel(part, ext_ref, slots_ref, wq_hbm, wk_hbm, wv_hbm, keep_ref, send_ref, w_ref, sems):
    span = w_ref.shape[0]
    step = span // PIECES
    copies = weight_copies(part, (wq_hbm, wk_hbm, wv_hbm), w_ref, sems)
    for copy in copies:
        copy.start()
    half = keep_ref.shape[0]
    slots = slots_ref.shape[0]
    hot = (ext_ref[:, 0:1].astype(F32) == iota((ext_ref.shape[0], slots), 1).astype(F32)).astype(BF16)
    held = dot(hot, slots_ref[...], ((1,), (0,))).astype(BF16)
    for j in range(PIECES):
        for copy in copies[3 * j : 3 * j + 3]:
            copy.wait()
        at = slice(j * step, (j + 1) * step)
        term = dot(held, w_ref[at, :], ((1,), (1,))).astype(BF16)
        keep_ref[:, at] = term[0:half]
        send_ref[:, at] = term[half:]


def back(part, ext, slot_grads, weights):
    rows = ext.shape[0]
    width = weights[0].shape[0]
    span = width // PARTS
    cols = sum(w.shape[1] for w in weights)
    out = jax.ShapeDtypeStruct((rows // 2, span), BF16)
    return pl.pallas_call(
        lambda *refs: back_kernel(part, *refs),
        in_specs=[VMEM, VMEM] + [ANY] * 3,
        out_specs=[VMEM] * 2,
        out_shape=[out, out],
        scratch_shapes=[pltpu.VMEM((span, cols), BF16), pltpu.SemaphoreType.DMA((3 * PIECES,))],
        compiler_params=params(20),
        cost_estimate=pl.CostEstimate(
            flops=2 * rows * span * cols, bytes_accessed=2 * span * cols, transcendentals=0
        ),
        name="back",
    )(ext, slot_grads, *[in_hbm(w) for w in weights])


def finish_kernel(hidden_ref, gain_ref, *refs):
    out_ref = refs[-1]
    wide = hidden_ref[...].astype(F32)
    inverse = lax.rsqrt(jnp.mean(wide * wide, axis=1, keepdims=True) + EPSILON)
    parts = []
    for i in range(PARTS):
        a, b, c = refs[3 * i : 3 * i + 3]
        parts.append(a[...].astype(F32) + b[...].astype(F32) + c[...].astype(F32))
    scaled = jnp.concatenate(parts, axis=1) * gain_ref[...]
    inner = jnp.mean(scaled * wide, axis=1, keepdims=True)
    out_ref[...] = (inverse * scaled - wide * inverse * inverse * inverse * inner).astype(BF16)


def on_device(hidden, gain, w_query, w_key, w_value, out_grad, owner, completion, rewards):
    groups = lax.axis_size("dp")
    ranks = lax.axis_size("tensor")
    chips = ranks // 2
    count, width = hidden.shape
    query_cols = w_query.shape[1]
    slots = 2 * groups * ranks
    span = width // PARTS

    swap_pairs = [(t, t ^ 1) for t in range(ranks)]
    flow_pairs = [(t, (t // 2 + (1 if t % 2 == 0 else chips - 1)) % chips * 2 + t % 2) for t in range(ranks)]

    def swap(x):
        return lax.ppermute(x, "tensor", swap_pairs)

    def flow(x):
        return lax.ppermute(x, "tensor", flow_pairs)

    near_cols = HEADS_AT + 2 * query_cols

    def rows_of(cols):
        return jax.ShapeDtypeStruct((count, cols), BF16)

    leave, cross, own = pl.pallas_call(
        norm_kernel,
        in_specs=[ANY] * 5,
        out_specs=[VMEM] * 3,
        out_shape=[rows_of(near_cols + 2 * query_cols), rows_of(near_cols + query_cols), rows_of(query_cols)],
        scratch_shapes=[
            pltpu.VMEM((count, width), BF16),
            pltpu.VMEM((1, width), F32),
            pltpu.VMEM((1, count), jnp.int32),
            pltpu.VMEM((1, count), jnp.int32),
            pltpu.VMEM((count, width), BF16),
            pltpu.SemaphoreType.DMA((5,)),
        ],
        compiler_params=params(),
        name="norm",
    )(
        *[
            in_hbm(x)
            for x in (hidden, gain.reshape(1, width), owner.reshape(1, count), completion.reshape(1, count), out_grad)
        ]
    )
    other = swap(cross)
    mine, leave_o = pl.pallas_call(
        join_kernel,
        in_specs=[VMEM] * 2,
        out_specs=[VMEM] * 2,
        out_shape=[rows_of(near_cols + 2 * query_cols), rows_of(near_cols)],
        compiler_params=params(),
        name="join",
    )(leave, other)

    weights = (w_query, w_key, w_value)
    near = flow(mine)
    near_o = flow(leave_o)
    first, ready = load(0, weights, leave_o)
    half_rows = rows_of(HEADS_AT + query_cols)
    passed, half_near = pl.pallas_call(
        relay_kernel,
        in_specs=[VMEM] * 2,
        out_specs=[VMEM] * 2,
        out_shape=[rows_of(near_cols), half_rows],
        compiler_params=params(),
        name="relay",
    )(near, ready)
    far = flow(passed)
    second, ready_too = load(1, weights, passed)

    def half_of(rows, after):
        return pl.pallas_call(
            half_kernel,
            in_specs=[VMEM] * 2,
            out_specs=VMEM,
            out_shape=half_rows,
            compiler_params=params(),
            name="half",
        )(rows, after)

    across = swap(half_near)
    across_o = swap(half_of(near_o, ready))
    far_o = swap(half_of(far, ready_too))
    blocks = (mine, other, near, near_o, across, across_o, far, far_o)
    loaded = (first, second)
    total, ext = project(blocks, loaded, own, slots)
    got = lax.all_to_all(
        total.reshape(groups, 2 * ranks, total.shape[1]), "dp", split_axis=0, concat_axis=0, tiled=True
    ).reshape(total.shape)

    cols = sum(w.shape[1] for w in weights)
    grads = pl.pallas_call(
        attend_kernel,
        in_specs=[VMEM] * 2,
        out_specs=VMEM,
        out_shape=jax.ShapeDtypeStruct((slots, cols), BF16),
        compiler_params=params(),
        name="attend",
    )(got, rewards)
    slot_grads = lax.all_to_all(
        grads.reshape(groups, 2 * ranks, cols), "dp", split_axis=0, concat_axis=0, tiled=True
    ).reshape(grads.shape)

    pieces = []
    for i in range(PARTS):
        keep, send = back(i, ext, slot_grads, weights)
        both = (keep.astype(F32) + swap(send).astype(F32)).astype(BF16)
        passed = flow(both[3 * count :])
        onward = both[count : 3 * count]
        onward = jnp.concatenate(
            [onward[:count], (onward[count:].astype(F32) + passed.astype(F32)).astype(BF16)], axis=0
        )
        came = flow(onward)
        pieces += [both[:count], came[count:], swap(came[:count])]

    return pl.pallas_call(
        finish_kernel,
        in_specs=[VMEM] * (2 + len(pieces)),
        out_specs=VMEM,
        out_shape=jax.ShapeDtypeStruct((count, width), BF16),
        compiler_params=params(),
        name="finish",
    )(hidden, gain.reshape(1, width), *pieces)


def solution(mesh):
    return jax.shard_map(
        on_device,
        mesh=mesh,
        in_specs=(
            P(("dp", "tensor"), None),
            P(),
            P(None, "tensor"),
            P(None, "tensor"),
            P(None, "tensor"),
            P(("dp", "tensor"), None),
            P(("dp", "tensor"), None),
            P(("dp", "tensor")),
            P("dp", None),
        ),
        out_specs=P(("dp", "tensor"), None),
        check_vma=False,
    )
```

```python
import jax
import jax.numpy as jnp
from jax import lax
from jax.experimental import pallas as pl
from jax.experimental.pallas import tpu as pltpu
from jax.sharding import PartitionSpec as P

HD = 128
KC = 16
PARTS = 2
EXT = 128
HEADS_AT = 8192 + EXT
STEP = 1024
PIECES = 4
EPSILON = 1e-05
BASE = 500000.0
F32 = jnp.float32
BF16 = jnp.bfloat16

TOKEN = jax.ShapeDtypeStruct((8, 128), F32)
VMEM = pl.BlockSpec(memory_space=pltpu.VMEM)
ANY = pl.BlockSpec(memory_space=pl.ANY)


def params(mib=12):
    return pltpu.CompilerParams(vmem_limit_bytes=mib * 2**20)


def in_hbm(x):
    return pltpu.with_memory_space_constraint(x, pltpu.HBM)


def in_vmem(x):
    return pltpu.with_memory_space_constraint(x, pltpu.VMEM)


def dot(a, b, dims):
    return lax.dot_general(a, b, (dims, ((), ())), preferred_element_type=F32)


def iota(shape, axis):
    return lax.broadcasted_iota(jnp.int32, shape, axis)


def chip_and_core():
    here = lax.axis_index("tensor")
    return here // 2, here % 2, lax.axis_size("tensor") // 2


def norm_kernel(hidden_hbm, gain_hbm, owner_hbm, completion_hbm, grad_hbm, leave_ref, cross_ref, next_ref, own_ref, *rest):
    hidden_ref, gain_ref, owner_ref, completion_ref, grad_ref, sems = rest
    copies = [
        pltpu.make_async_copy(src, dst, sems.at[i])
        for i, (src, dst) in enumerate(
            (
                (hidden_hbm, hidden_ref),
                (gain_hbm, gain_ref),
                (owner_hbm, owner_ref),
                (completion_hbm, completion_ref),
                (grad_hbm, grad_ref),
            )
        )
    ]
    for copy in copies:
        copy.start()
    for copy in copies:
        copy.wait()
    count, width = hidden_ref.shape
    wide = hidden_ref[...].astype(F32)
    inverse = lax.rsqrt(jnp.mean(wide * wide, axis=1, keepdims=True) + EPSILON)
    rows, cols = iota((count, count), 0), iota((count, count), 1)
    owner_row = owner_ref[...].astype(F32)
    owner = jnp.sum(jnp.where(rows == cols, owner_row, 0.0), axis=1, keepdims=True)
    label = jnp.sum(
        jnp.where(rows == cols, completion_ref[...].astype(F32) + 1.0, 0.0), axis=1, keepdims=True
    )
    rank = jnp.sum(jnp.where((owner == owner_row) & (cols < rows), 1.0, 0.0), axis=1, keepdims=True)
    here = lax.axis_index("tensor").astype(F32)
    slot = owner * 16.0 + here * 2.0 + rank
    lane = iota((count, EXT), 1)
    ext = jnp.where(lane == 0, slot, jnp.where(lane == 1, label, 0.0)).astype(BF16)
    normed = (wide * inverse * gain_ref[...]).astype(BF16)
    for ref in (leave_ref, cross_ref):
        ref[:, 0:width] = normed
        ref[:, width : width + EXT] = ext
    chip, core, chips = chip_and_core()
    each = own_ref.shape[1]

    def heads(at, n):
        return grad_ref[:, pl.ds(pl.multiple_of(at * each, each), n * each)]

    up, down = (chip + 1) % chips, (chip + chips - 1) % chips
    at = width + EXT
    leave_ref[:, at:] = heads(2 * ((chip + 2) % chips), 2)
    next_ref[...] = heads(2 * jnp.where(core == 0, up, down), 2)
    cross_ref[:, at : at + 2 * each] = heads(2 * jnp.where(core == 0, down, up), 2)
    cross_ref[:, at + 2 * each :] = heads(2 * chip + 1 - core, 1)
    own_ref[...] = heads(2 * chip + core, 1)


def join_kernel(other_ref, next_ref, out_ref):
    n = out_ref.shape[1] - next_ref.shape[1]
    out_ref[:, 0:n] = other_ref[:, 0:n]
    out_ref[:, n:] = next_ref[...]


def half(rows_ref, heads_ref, at, out_ref):
    n = HEADS_AT
    each = out_ref.shape[1] - n
    _, core, _ = chip_and_core()
    out_ref[:, 0:n] = rows_ref[:, 0:n]
    first, second = heads_ref[:, at : at + each], heads_ref[:, at + each : at + 2 * each]
    out_ref[:, n:] = jnp.where(core == 0, second, first)


def half_near_kernel(near_ref, near_o_ref, _, out_ref, out_o_ref):
    each = out_ref.shape[1] - HEADS_AT
    half(near_ref, near_o_ref, HEADS_AT + 2 * each, out_ref)
    half(near_o_ref, near_o_ref, HEADS_AT, out_o_ref)


def half_far_kernel(far_ref, _, out_ref):
    half(far_ref, far_ref, HEADS_AT, out_ref)


def relay_kernel(near_ref, _, out_ref):
    out_ref[...] = near_ref[...]


def load_kernel(part, wq_hbm, wk_hbm, wv_hbm, _, out_ref, token_ref, sems):
    token_ref[...] = jnp.zeros_like(token_ref)
    span = out_ref.shape[0]
    step = span // PIECES
    copies = []
    at = 0
    for w in (wq_hbm, wk_hbm, wv_hbm):
        n = w.shape[1]
        for j in range(PIECES):
            copies.append(
                pltpu.make_async_copy(
                    w.at[pl.ds(part * span + j * step, step), :],
                    out_ref.at[pl.ds(j * step, step), pl.ds(at, n)],
                    sems.at[len(copies)],
                )
            )
        at += n
    for copy in copies:
        copy.start()
    for copy in copies:
        copy.wait()


def load(part, weights, after):
    span = weights[0].shape[0] // PARTS
    cols = sum(w.shape[1] for w in weights)
    return pl.pallas_call(
        lambda *refs: load_kernel(part, *refs),
        in_specs=[ANY] * 3 + [VMEM],
        out_specs=[VMEM] * 2,
        out_shape=[pltpu.VMEM((span, cols), BF16), TOKEN],
        scratch_shapes=[pltpu.SemaphoreType.DMA((3 * PIECES,))],
        compiler_params=params(),
        cost_estimate=pl.CostEstimate(flops=0, bytes_accessed=2 * span * cols, transcendentals=0),
        name="load",
    )(*[in_hbm(w) for w in weights], after)


def project_kernel(count, *refs):
    blocks = refs[:count]
    parts = refs[count : count + PARTS]
    own_ref, out_ref, ext_ref, x_ref = refs[count + PARTS :]
    width = x_ref.shape[1]
    rows = blocks[0].shape[0]
    for i, b in enumerate(blocks):
        x_ref[i * rows : (i + 1) * rows, :] = b[:, 0:width]
    exts = [b[:, width : width + EXT] for b in blocks]
    mine, other, near, near_o, across, across_o, far, far_o = exts
    ext_ref[...] = jnp.concatenate([mine, across, across_o, far, other, near, near_o, far_o], axis=0)
    total = None
    for i, w in enumerate(parts):
        span = w.shape[0]
        value = dot(x_ref[:, i * span : (i + 1) * span], w[...], ((1,), (0,)))
        total = value if total is None else total + value
    total = total.astype(BF16)
    cols = total.shape[1]
    slots = out_ref.shape[0]
    ext = jnp.concatenate(exts, axis=0)
    spread = (ext[:, 0:1].astype(F32) == iota((ext.shape[0], slots), 1).astype(F32)).astype(BF16)
    out_ref[:, 0:cols] = dot(spread, total, ((0,), (0,))).astype(BF16)
    out_ref[:, cols : cols + EXT] = dot(spread, ext, ((0,), (0,))).astype(BF16)
    _, core, _ = chip_and_core()
    n = HEADS_AT
    each = own_ref.shape[1]

    def heads(b, at):
        return jnp.where(core == 0, b[:, at : at + each], b[:, at + each : at + 2 * each])

    mine, other, near, near_o, across, across_o, far, far_o = blocks
    grads = [own_ref[...], other[:, n + 2 * each :], heads(near_o, n + 2 * each), heads(near_o, n)]
    grads += [across[:, n:], across_o[:, n:], heads(far, n), far_o[:, n:]]
    out_ref[:, cols + EXT :] = dot(spread, jnp.concatenate(grads, axis=0), ((0,), (0,))).astype(BF16)


def project(blocks, loaded, own, slots):
    rows = sum(b.shape[0] for b in blocks)
    span, cols = loaded[0].shape
    width = span * PARTS
    return pl.pallas_call(
        lambda *refs: project_kernel(len(blocks), *refs),
        in_specs=[VMEM] * (len(blocks) + PARTS + 1),
        out_specs=[VMEM] * 2,
        out_shape=[
            jax.ShapeDtypeStruct((slots, cols + EXT + own.shape[1]), BF16),
            jax.ShapeDtypeStruct((rows, EXT), BF16),
        ],
        scratch_shapes=[pltpu.VMEM((rows, width), BF16)],
        compiler_params=params(),
        cost_estimate=pl.CostEstimate(
            flops=2 * rows * width * cols, bytes_accessed=2 * width * cols, transcendentals=0
        ),
        name="project",
    )(*blocks, *[in_vmem(w) for w in loaded], own)


def attend_kernel(got_ref, rewards_ref, out_ref):
    slots = got_ref.shape[0]
    heads = out_ref.shape[1] // HD - 2
    kcol = heads * HD
    vcol = kcol + HD
    ecol = vcol + HD
    gcol = ecol + EXT
    factor = HD**-0.5
    ext = got_ref[:, ecol : ecol + EXT].astype(F32)
    label = ext[:, 1:2]
    label_row = jnp.transpose(ext)[1:2, :]
    rows, cols = iota((slots, slots), 0), iota((slots, slots), 1)
    same = label == label_row
    bias = jnp.where(same & (rows <= cols), 0.0, -1e30)
    position = jnp.sum(jnp.where(same & (cols < rows), 1.0, 0.0), axis=1, keepdims=True)
    lane = iota((slots, HD), 1)
    half = HD // 2
    index = jnp.where(lane < half, lane, lane - half).astype(F32)
    freq = jnp.exp(index * (-2.0 / HD * jnp.log(F32(BASE))))
    angle = position * freq
    cosine = jnp.cos(angle)
    sine = jnp.sin(angle)
    sine = jnp.where(lane < half, -sine, sine)

    def rope(u):
        return u * cosine + pltpu.roll(u, half, 1) * sine

    def rope_back(u):
        return u * cosine - pltpu.roll(u, half, 1) * sine

    scaled = rewards_ref[...].astype(F32) / 256.0
    advantage = scaled - (jnp.sum(scaled) - scaled) / (KC - 1)
    advantage = jnp.concatenate([advantage, jnp.zeros((1, EXT - KC), F32)], axis=1)
    weight = jnp.sum(jnp.where(label - 1.0 == lane.astype(F32), advantage, 0.0), axis=1, keepdims=True)

    key = rope(got_ref[:, kcol : kcol + HD].astype(F32)).astype(BF16)
    value = got_ref[:, vcol : vcol + HD]
    grad_key = jnp.zeros((slots, HD), F32)
    grad_value = jnp.zeros((slots, HD), F32)
    for h in range(heads):
        at = slice(h * HD, (h + 1) * HD)
        query = rope(got_ref[:, at].astype(F32)).astype(BF16)
        grad = (got_ref[:, gcol + h * HD : gcol + (h + 1) * HD].astype(F32) * weight).astype(BF16)
        scores = dot(key, query, ((1,), (1,))) * factor + bias
        highest = jnp.max(scores, axis=0, keepdims=True)
        weights = jnp.exp(scores - highest)
        probs = weights * (1.0 / jnp.sum(weights, axis=0, keepdims=True))
        grad_value = grad_value + dot(probs.astype(BF16), grad, ((1,), (0,)))
        grad_probs = dot(value, grad, ((1,), (1,)))
        inner = jnp.sum(probs * grad_probs, axis=0, keepdims=True)
        grad_scores = (probs * (grad_probs - inner) * factor).astype(BF16)
        grad_query = dot(grad_scores, key, ((0,), (0,)))
        grad_key = grad_key + dot(grad_scores, query, ((1,), (0,)))
        out_ref[:, at] = rope_back(grad_query).astype(BF16)
    out_ref[:, kcol : kcol + HD] = rope_back(grad_key).astype(BF16)
    out_ref[:, vcol : vcol + HD] = grad_value.astype(BF16)


def back_kernel(ext_ref, slots_ref, w_ref, keep_ref, send_ref):
    half_rows, span = keep_ref.shape
    slots = slots_ref.shape[0]
    hot = (ext_ref[:, 0:1].astype(F32) == iota((ext_ref.shape[0], slots), 1).astype(F32)).astype(BF16)
    held = dot(hot, slots_ref[...], ((1,), (0,))).astype(BF16)
    for j in range(span // STEP):
        at = slice(j * STEP, (j + 1) * STEP)
        term = dot(held, w_ref[at, :], ((1,), (1,))).astype(BF16)
        keep_ref[:, at] = term[0:half_rows]
        send_ref[:, at] = term[half_rows:]


def back(ext, slot_grads, w):
    rows = ext.shape[0]
    span, cols = w.shape
    out = jax.ShapeDtypeStruct((rows // 2, span), BF16)
    return pl.pallas_call(
        back_kernel,
        in_specs=[VMEM] * 3,
        out_specs=[VMEM] * 2,
        out_shape=[out, out],
        compiler_params=params(),
        cost_estimate=pl.CostEstimate(
            flops=2 * rows * span * cols, bytes_accessed=2 * span * cols, transcendentals=0
        ),
        name="back",
    )(ext, slot_grads, in_vmem(w))


def finish_kernel(counts, hidden_ref, gain_ref, *refs):
    out_ref = refs[-1]
    wide = hidden_ref[...].astype(F32)
    inverse = lax.rsqrt(jnp.mean(wide * wide, axis=1, keepdims=True) + EPSILON)
    parts = []
    at = 0
    for n in counts:
        parts.append(sum(ref[...].astype(F32) for ref in refs[at : at + n]))
        at += n
    scaled = jnp.concatenate(parts, axis=1) * gain_ref[...]
    inner = jnp.mean(scaled * wide, axis=1, keepdims=True)
    out_ref[...] = (inverse * scaled - wide * inverse * inverse * inverse * inner).astype(BF16)


def on_device(hidden, gain, w_query, w_key, w_value, out_grad, owner, completion, rewards):
    groups = lax.axis_size("dp")
    ranks = lax.axis_size("tensor")
    chips = ranks // 2
    count, width = hidden.shape
    query_cols = w_query.shape[1]
    slots = 2 * groups * ranks
    span = width // PARTS

    swap_pairs = [(t, t ^ 1) for t in range(ranks)]
    flow_pairs = [(t, (t // 2 + (1 if t % 2 == 0 else chips - 1)) % chips * 2 + t % 2) for t in range(ranks)]

    def swap(x):
        return lax.ppermute(x, "tensor", swap_pairs)

    def flow(x):
        return lax.ppermute(x, "tensor", flow_pairs)

    near_cols = HEADS_AT + 2 * query_cols

    def rows_of(cols):
        return jax.ShapeDtypeStruct((count, cols), BF16)

    leave, cross, onto_next, own = pl.pallas_call(
        norm_kernel,
        in_specs=[ANY] * 5,
        out_specs=[VMEM] * 4,
        out_shape=[rows_of(n) for n in (near_cols, near_cols + query_cols, 2 * query_cols, query_cols)],
        scratch_shapes=[
            pltpu.VMEM((count, width), BF16),
            pltpu.VMEM((1, width), F32),
            pltpu.VMEM((1, count), jnp.int32),
            pltpu.VMEM((1, count), jnp.int32),
            pltpu.VMEM((count, width), BF16),
            pltpu.SemaphoreType.DMA((5,)),
        ],
        compiler_params=params(),
        name="norm",
    )(
        *[
            in_hbm(x)
            for x in (hidden, gain.reshape(1, width), owner.reshape(1, count), completion.reshape(1, count), out_grad)
        ]
    )
    near = flow(leave)
    other = swap(cross)
    leave_o = pl.pallas_call(
        join_kernel,
        in_specs=[VMEM] * 2,
        out_specs=VMEM,
        out_shape=rows_of(near_cols + 2 * query_cols),
        compiler_params=params(),
        name="join",
    )(other, onto_next)

    weights = (w_query, w_key, w_value)
    near_o = flow(leave_o)
    first, ready = load(0, weights, leave_o)
    passed = pl.pallas_call(
        relay_kernel,
        in_specs=[VMEM] * 2,
        out_specs=VMEM,
        out_shape=rows_of(near_cols),
        compiler_params=params(),
        name="relay",
    )(near, ready)
    far = flow(passed)
    second, ready_too = load(1, weights, passed)

    half_rows = rows_of(HEADS_AT + query_cols)
    half_near, half_near_o = pl.pallas_call(
        half_near_kernel,
        in_specs=[VMEM] * 3,
        out_specs=[VMEM] * 2,
        out_shape=[half_rows] * 2,
        compiler_params=params(),
        name="half_near",
    )(near, near_o, ready_too)
    half_far = pl.pallas_call(
        half_far_kernel,
        in_specs=[VMEM] * 2,
        out_specs=VMEM,
        out_shape=half_rows,
        compiler_params=params(),
        name="half_far",
    )(far, ready_too)
    blocks = (leave, other, near, near_o, swap(half_near), swap(half_near_o), far, swap(half_far))
    loaded = (first, second)
    total, ext = project(blocks, loaded, own, slots)
    got = lax.all_to_all(
        total.reshape(groups, 2 * ranks, total.shape[1]), "dp", split_axis=0, concat_axis=0, tiled=True
    ).reshape(total.shape)

    cols = sum(w.shape[1] for w in weights)
    grads = pl.pallas_call(
        attend_kernel,
        in_specs=[VMEM] * 2,
        out_specs=VMEM,
        out_shape=jax.ShapeDtypeStruct((slots, cols), BF16),
        compiler_params=params(),
        name="attend",
    )(got, rewards)
    slot_grads = lax.all_to_all(
        grads.reshape(groups, 2 * ranks, cols), "dp", split_axis=0, concat_axis=0, tiled=True
    ).reshape(grads.shape)

    def add(a, b):
        return (a.astype(F32) + b.astype(F32)).astype(BF16)

    pieces = []
    for i in range(PARTS):
        keep, send = back(ext, slot_grads, loaded[i])
        both = add(keep, swap(send))
        mine, onward = both[:count], both[count : 3 * count]
        passed = flow(both[3 * count :])
        if i < PARTS - 1:
            came = flow(onward)
            mine = (mine, flow(passed))
        else:
            came = flow(jnp.concatenate([onward[:count], add(onward[count:], passed)], axis=0))
            mine = (mine,)
        pieces.append((*mine, came[count:], swap(came[:count])))
    counts = [len(p) for p in pieces]
    pieces = [x for p in pieces for x in p]

    return pl.pallas_call(
        lambda *refs: finish_kernel(counts, *refs),
        in_specs=[VMEM] * (2 + len(pieces)),
        out_specs=VMEM,
        out_shape=jax.ShapeDtypeStruct((count, width), BF16),
        compiler_params=params(),
        name="finish",
    )(hidden, gain.reshape(1, width), *pieces)


def solution(mesh):
    return jax.shard_map(
        on_device,
        mesh=mesh,
        in_specs=(
            P(("dp", "tensor"), None),
            P(),
            P(None, "tensor"),
            P(None, "tensor"),
            P(None, "tensor"),
            P(("dp", "tensor"), None),
            P(("dp", "tensor"), None),
            P(("dp", "tensor")),
            P("dp", None),
        ),
        out_specs=P(("dp", "tensor"), None),
        check_vma=False,
    )
```

```python
import jax
import jax.numpy as jnp
from jax import lax
from jax.experimental import pallas as pl
from jax.experimental.pallas import tpu as pltpu
from jax.sharding import PartitionSpec as P

HD = 128
KC = 16
PARTS = 2
EXT = 128
HEADS_AT = 8192 + EXT
STEP = 1024
PIECES = 4
TURN = 512
EPSILON = 1e-05
BASE = 500000.0
F32 = jnp.float32
BF16 = jnp.bfloat16

TOKEN = jax.ShapeDtypeStruct((8, 128), F32)
VMEM = pl.BlockSpec(memory_space=pltpu.VMEM)
ANY = pl.BlockSpec(memory_space=pl.ANY)


def params(mib=8):
    return pltpu.CompilerParams(vmem_limit_bytes=mib * 2**20)


def in_hbm(x):
    return pltpu.with_memory_space_constraint(x, pltpu.HBM)


def in_vmem(x):
    return pltpu.with_memory_space_constraint(x, pltpu.VMEM)


def dot(a, b, dims):
    return lax.dot_general(a, b, (dims, ((), ())), preferred_element_type=F32)


def iota(shape, axis):
    return lax.broadcasted_iota(jnp.int32, shape, axis)


def chip_and_core():
    here = lax.axis_index("tensor")
    return here // 2, here % 2, lax.axis_size("tensor") // 2


def norm_kernel(hidden_hbm, gain_hbm, owner_hbm, completion_hbm, grad_hbm, leave_ref, cross_ref, next_ref, own_ref, *rest):
    hidden_ref, gain_ref, owner_ref, completion_ref, grad_ref, sems = rest
    copies = [
        pltpu.make_async_copy(src, dst, sems.at[i])
        for i, (src, dst) in enumerate(
            (
                (hidden_hbm, hidden_ref),
                (gain_hbm, gain_ref),
                (owner_hbm, owner_ref),
                (completion_hbm, completion_ref),
                (grad_hbm, grad_ref),
            )
        )
    ]
    for copy in copies:
        copy.start()
    for copy in copies:
        copy.wait()
    count, width = hidden_ref.shape
    wide = hidden_ref[...].astype(F32)
    inverse = lax.rsqrt(jnp.mean(wide * wide, axis=1, keepdims=True) + EPSILON)
    rows, cols = iota((count, count), 0), iota((count, count), 1)
    owner_row = owner_ref[...].astype(F32)
    owner = jnp.sum(jnp.where(rows == cols, owner_row, 0.0), axis=1, keepdims=True)
    label = jnp.sum(
        jnp.where(rows == cols, completion_ref[...].astype(F32) + 1.0, 0.0), axis=1, keepdims=True
    )
    rank = jnp.sum(jnp.where((owner == owner_row) & (cols < rows), 1.0, 0.0), axis=1, keepdims=True)
    here = lax.axis_index("tensor").astype(F32)
    slot = owner * 16.0 + here * 2.0 + rank
    lane = iota((count, EXT), 1)
    ext = jnp.where(lane == 0, slot, jnp.where(lane == 1, label, 0.0)).astype(BF16)
    normed = (wide * inverse * gain_ref[...]).astype(BF16)
    for ref in (leave_ref, cross_ref):
        ref[:, 0:width] = normed
        ref[:, width : width + EXT] = ext
    chip, core, chips = chip_and_core()
    each = own_ref.shape[1]

    def heads(at, n):
        return grad_ref[:, pl.ds(pl.multiple_of(at * each, each), n * each)]

    up, down = (chip + 1) % chips, (chip + chips - 1) % chips
    at = width + EXT
    leave_ref[:, at:] = heads(2 * ((chip + 2) % chips), 2)
    next_ref[...] = heads(2 * jnp.where(core == 0, up, down), 2)
    cross_ref[:, at : at + 2 * each] = heads(2 * jnp.where(core == 0, down, up), 2)
    cross_ref[:, at + 2 * each :] = heads(2 * chip + 1 - core, 1)
    own_ref[...] = heads(2 * chip + core, 1)


def join_kernel(other_ref, next_ref, out_ref):
    n = out_ref.shape[1] - next_ref.shape[1]
    out_ref[:, 0:n] = other_ref[:, 0:n]
    out_ref[:, n:] = next_ref[...]


def half(rows_ref, heads_ref, at, out_ref):
    n = HEADS_AT
    each = out_ref.shape[1] - n
    _, core, _ = chip_and_core()
    out_ref[:, 0:n] = rows_ref[:, 0:n]
    first, second = heads_ref[:, at : at + each], heads_ref[:, at + each : at + 2 * each]
    out_ref[:, n:] = jnp.where(core == 0, second, first)


def half_near_kernel(near_ref, near_o_ref, _, out_ref, out_o_ref):
    each = out_ref.shape[1] - HEADS_AT
    half(near_ref, near_o_ref, HEADS_AT + 2 * each, out_ref)
    half(near_o_ref, near_o_ref, HEADS_AT, out_o_ref)


def half_far_kernel(far_ref, _, out_ref):
    half(far_ref, far_ref, HEADS_AT, out_ref)


def relay_kernel(near_ref, _, out_ref):
    out_ref[...] = near_ref[...]


def load_kernel(part, wq_hbm, wk_hbm, wv_hbm, _, out_ref, token_ref, *rest):
    turned_ref, sems = rest[0], rest[-1]
    token_ref[...] = jnp.zeros_like(token_ref)
    span = out_ref.shape[0]
    step = span // PIECES
    copies = []
    for j in range(PIECES):
        at = 0
        for w in (wq_hbm, wk_hbm, wv_hbm):
            n = w.shape[1]
            copies.append(
                pltpu.make_async_copy(
                    w.at[pl.ds(part * span + j * step, step), :],
                    out_ref.at[pl.ds(j * step, step), pl.ds(at, n)],
                    sems.at[len(copies)],
                )
            )
            at += n
    for copy in copies:
        copy.start()
    for j in range(PIECES):
        for copy in copies[3 * j : 3 * j + 3]:
            copy.wait()
        if part == 0:
            continue

        @pl.loop(0, step // TURN)
        def _(k):
            at = pl.ds(pl.multiple_of(j * step + k * TURN, TURN), TURN)
            turned_ref[:, at] = jnp.transpose(out_ref[at, :])


def load(part, weights, after):
    span = weights[0].shape[0] // PARTS
    cols = sum(w.shape[1] for w in weights)
    return pl.pallas_call(
        lambda *refs: load_kernel(part, *refs),
        in_specs=[ANY] * 3 + [VMEM],
        out_specs=[VMEM] * (2 + (part > 0)),
        out_shape=[pltpu.VMEM((span, cols), BF16), TOKEN] + [pltpu.VMEM((cols, span), BF16)] * (part > 0),
        scratch_shapes=[pltpu.SemaphoreType.DMA((3 * PIECES,))],
        compiler_params=params(),
        cost_estimate=pl.CostEstimate(flops=0, bytes_accessed=2 * span * cols, transcendentals=0),
        name="load",
    )(*[in_hbm(w) for w in weights], after)


def project_kernel(count, *refs):
    blocks = refs[:count]
    parts = refs[count : count + PARTS]
    own_ref, out_ref, ext_ref, x_ref = refs[count + PARTS :]
    width = x_ref.shape[1]
    rows = blocks[0].shape[0]
    for i, b in enumerate(blocks):
        x_ref[i * rows : (i + 1) * rows, :] = b[:, 0:width]
    exts = [b[:, width : width + EXT] for b in blocks]
    mine, other, near, near_o, across, across_o, far, far_o = exts
    ext_ref[...] = jnp.concatenate([mine, across, across_o, far, other, near, near_o, far_o], axis=0)
    total = None
    for i, w in enumerate(parts):
        span = w.shape[0]
        value = dot(x_ref[:, i * span : (i + 1) * span], w[...], ((1,), (0,)))
        total = value if total is None else total + value
    total = total.astype(BF16)
    cols = total.shape[1]
    slots = out_ref.shape[0]
    ext = jnp.concatenate(exts, axis=0)
    place = jnp.transpose(ext.astype(F32))[0:1, :]
    spread = (place == iota((slots, ext.shape[0]), 0).astype(F32)).astype(BF16)
    out_ref[:, 0:cols] = dot(spread, total, ((1,), (0,))).astype(BF16)
    out_ref[:, cols : cols + EXT] = dot(spread, ext, ((1,), (0,))).astype(BF16)
    _, core, _ = chip_and_core()
    n = HEADS_AT
    each = own_ref.shape[1]

    def heads(b, at):
        return jnp.where(core == 0, b[:, at : at + each], b[:, at + each : at + 2 * each])

    mine, other, near, near_o, across, across_o, far, far_o = blocks
    grads = [own_ref[...], other[:, n + 2 * each :], heads(near_o, n + 2 * each), heads(near_o, n)]
    grads += [across[:, n:], across_o[:, n:], heads(far, n), far_o[:, n:]]
    out_ref[:, cols + EXT :] = dot(spread, jnp.concatenate(grads, axis=0), ((1,), (0,))).astype(BF16)


def project(blocks, loaded, own, slots):
    rows = sum(b.shape[0] for b in blocks)
    span, cols = loaded[0].shape
    width = span * PARTS
    return pl.pallas_call(
        lambda *refs: project_kernel(len(blocks), *refs),
        in_specs=[VMEM] * (len(blocks) + PARTS + 1),
        out_specs=[VMEM] * 2,
        out_shape=[
            jax.ShapeDtypeStruct((slots, cols + EXT + own.shape[1]), BF16),
            jax.ShapeDtypeStruct((rows, EXT), BF16),
        ],
        scratch_shapes=[pltpu.VMEM((rows, width), BF16)],
        compiler_params=params(),
        cost_estimate=pl.CostEstimate(
            flops=2 * rows * width * cols, bytes_accessed=2 * width * cols, transcendentals=0
        ),
        name="project",
    )(*blocks, *[in_vmem(w) for w in loaded], own)


def attend_kernel(got_ref, rewards_ref, out_ref):
    slots = got_ref.shape[0]
    heads = out_ref.shape[1] // HD - 2
    kcol = heads * HD
    vcol = kcol + HD
    ecol = vcol + HD
    gcol = ecol + EXT
    factor = HD**-0.5
    ext = got_ref[:, ecol : ecol + EXT].astype(F32)
    label = ext[:, 1:2]
    label_row = jnp.transpose(ext)[1:2, :]
    rows, cols = iota((slots, slots), 0), iota((slots, slots), 1)
    same = label == label_row
    bias = jnp.where(same & (rows <= cols), 0.0, -1e30)
    position = jnp.sum(jnp.where(same & (cols < rows), 1.0, 0.0), axis=1, keepdims=True)
    lane = iota((slots, HD), 1)
    half = HD // 2
    index = jnp.where(lane < half, lane, lane - half).astype(F32)
    freq = jnp.exp(index * (-2.0 / HD * jnp.log(F32(BASE))))
    angle = position * freq
    cosine = jnp.cos(angle)
    sine = jnp.sin(angle)
    sine = jnp.where(lane < half, -sine, sine)

    def rope(u):
        return u * cosine + pltpu.roll(u, half, 1) * sine

    def rope_back(u):
        return u * cosine - pltpu.roll(u, half, 1) * sine

    scaled = rewards_ref[...].astype(F32) / 256.0
    advantage = scaled - (jnp.sum(scaled) - scaled) / (KC - 1)
    advantage = jnp.concatenate([advantage, jnp.zeros((1, EXT - KC), F32)], axis=1)
    weight = jnp.sum(jnp.where(label - 1.0 == lane.astype(F32), advantage, 0.0), axis=1, keepdims=True)

    key = rope(got_ref[:, kcol : kcol + HD].astype(F32)).astype(BF16)
    value = got_ref[:, vcol : vcol + HD]
    grad_key = jnp.zeros((slots, HD), F32)
    grad_value = jnp.zeros((slots, HD), F32)
    for h in range(heads):
        at = slice(h * HD, (h + 1) * HD)
        query = rope(got_ref[:, at].astype(F32)).astype(BF16)
        grad = (got_ref[:, gcol + h * HD : gcol + (h + 1) * HD].astype(F32) * weight).astype(BF16)
        scores = dot(key, query, ((1,), (1,))) * factor + bias
        highest = jnp.max(scores, axis=0, keepdims=True)
        weights = jnp.exp(scores - highest)
        probs = weights * (1.0 / jnp.sum(weights, axis=0, keepdims=True))
        grad_value = grad_value + dot(probs.astype(BF16), grad, ((1,), (0,)))
        grad_probs = dot(value, grad, ((1,), (1,)))
        inner = jnp.sum(probs * grad_probs, axis=0, keepdims=True)
        grad_scores = (probs * (grad_probs - inner) * factor).astype(BF16)
        grad_query = dot(grad_scores, key, ((0,), (0,)))
        grad_key = grad_key + dot(grad_scores, query, ((1,), (0,)))
        out_ref[:, at] = rope_back(grad_query).astype(BF16)
    out_ref[:, kcol : kcol + HD] = rope_back(grad_key).astype(BF16)
    out_ref[:, vcol : vcol + HD] = grad_value.astype(BF16)


def back_kernel(is_turned, ext_ref, slots_ref, w_ref, keep_ref, send_ref):
    half_rows, span = keep_ref.shape
    slots = slots_ref.shape[0]
    hot = (ext_ref[:, 0:1].astype(F32) == iota((ext_ref.shape[0], slots), 1).astype(F32)).astype(BF16)
    held = dot(hot, slots_ref[...], ((1,), (0,))).astype(BF16)
    for j in range(span // STEP):
        at = slice(j * STEP, (j + 1) * STEP)
        if is_turned:
            term = dot(held, w_ref[:, at], ((1,), (0,))).astype(BF16)
        else:
            term = dot(held, w_ref[at, :], ((1,), (1,))).astype(BF16)
        keep_ref[:, at] = term[0:half_rows]
        send_ref[:, at] = term[half_rows:]


def back(ext, slot_grads, w, is_turned):
    rows = ext.shape[0]
    cols, span = w.shape if is_turned else w.shape[::-1]
    out = jax.ShapeDtypeStruct((rows // 2, span), BF16)
    return pl.pallas_call(
        lambda *refs: back_kernel(is_turned, *refs),
        in_specs=[VMEM] * 3,
        out_specs=[VMEM] * 2,
        out_shape=[out, out],
        compiler_params=params(),
        cost_estimate=pl.CostEstimate(
            flops=2 * rows * span * cols, bytes_accessed=2 * span * cols, transcendentals=0
        ),
        name="back",
    )(ext, slot_grads, in_vmem(w))


def finish_kernel(counts, hidden_ref, gain_ref, *refs):
    out_ref = refs[-1]
    wide = hidden_ref[...].astype(F32)
    inverse = lax.rsqrt(jnp.mean(wide * wide, axis=1, keepdims=True) + EPSILON)
    parts = []
    at = 0
    for n in counts:
        parts.append(sum(ref[...].astype(F32) for ref in refs[at : at + n]))
        at += n
    scaled = jnp.concatenate(parts, axis=1) * gain_ref[...]
    inner = jnp.mean(scaled * wide, axis=1, keepdims=True)
    out_ref[...] = (inverse * scaled - wide * inverse * inverse * inverse * inner).astype(BF16)


def on_device(hidden, gain, w_query, w_key, w_value, out_grad, owner, completion, rewards):
    groups = lax.axis_size("dp")
    ranks = lax.axis_size("tensor")
    chips = ranks // 2
    count, width = hidden.shape
    query_cols = w_query.shape[1]
    slots = 2 * groups * ranks
    span = width // PARTS

    swap_pairs = [(t, t ^ 1) for t in range(ranks)]
    flow_pairs = [(t, (t // 2 + (1 if t % 2 == 0 else chips - 1)) % chips * 2 + t % 2) for t in range(ranks)]

    def swap(x):
        return lax.ppermute(x, "tensor", swap_pairs)

    def flow(x):
        return lax.ppermute(x, "tensor", flow_pairs)

    near_cols = HEADS_AT + 2 * query_cols

    def rows_of(cols):
        return jax.ShapeDtypeStruct((count, cols), BF16)

    leave, cross, onto_next, own = pl.pallas_call(
        norm_kernel,
        in_specs=[ANY] * 5,
        out_specs=[VMEM] * 4,
        out_shape=[rows_of(n) for n in (near_cols, near_cols + query_cols, 2 * query_cols, query_cols)],
        scratch_shapes=[
            pltpu.VMEM((count, width), BF16),
            pltpu.VMEM((1, width), F32),
            pltpu.VMEM((1, count), jnp.int32),
            pltpu.VMEM((1, count), jnp.int32),
            pltpu.VMEM((count, width), BF16),
            pltpu.SemaphoreType.DMA((5,)),
        ],
        compiler_params=params(),
        name="norm",
    )(
        *[
            in_hbm(x)
            for x in (hidden, gain.reshape(1, width), owner.reshape(1, count), completion.reshape(1, count), out_grad)
        ]
    )
    near = flow(leave)
    other = swap(cross)
    leave_o = pl.pallas_call(
        join_kernel,
        in_specs=[VMEM] * 2,
        out_specs=VMEM,
        out_shape=rows_of(near_cols + 2 * query_cols),
        compiler_params=params(),
        name="join",
    )(other, onto_next)

    weights = (w_query, w_key, w_value)
    near_o = flow(leave_o)
    first, ready = load(0, weights, leave_o)
    passed = pl.pallas_call(
        relay_kernel,
        in_specs=[VMEM] * 2,
        out_specs=VMEM,
        out_shape=rows_of(near_cols),
        compiler_params=params(),
        name="relay",
    )(near, ready)
    far = flow(passed)
    second, ready_too, turned = load(1, weights, passed)

    half_rows = rows_of(HEADS_AT + query_cols)
    half_near, half_near_o = pl.pallas_call(
        half_near_kernel,
        in_specs=[VMEM] * 3,
        out_specs=[VMEM] * 2,
        out_shape=[half_rows] * 2,
        compiler_params=params(),
        name="half_near",
    )(near, near_o, ready_too)
    half_far = pl.pallas_call(
        half_far_kernel,
        in_specs=[VMEM] * 2,
        out_specs=VMEM,
        out_shape=half_rows,
        compiler_params=params(),
        name="half_far",
    )(far, ready_too)
    blocks = (leave, other, near, near_o, swap(half_near), swap(half_near_o), far, swap(half_far))
    loaded = (first, second)
    total, ext = project(blocks, loaded, own, slots)
    got = lax.all_to_all(
        total.reshape(groups, 2 * ranks, total.shape[1]), "dp", split_axis=0, concat_axis=0, tiled=True
    ).reshape(total.shape)

    cols = sum(w.shape[1] for w in weights)
    grads = pl.pallas_call(
        attend_kernel,
        in_specs=[VMEM] * 2,
        out_specs=VMEM,
        out_shape=jax.ShapeDtypeStruct((slots, cols), BF16),
        compiler_params=params(),
        name="attend",
    )(got, rewards)
    slot_grads = lax.all_to_all(
        grads.reshape(groups, 2 * ranks, cols), "dp", split_axis=0, concat_axis=0, tiled=True
    ).reshape(grads.shape)

    def add(a, b):
        return (a.astype(F32) + b.astype(F32)).astype(BF16)

    pieces = []
    for i in range(PARTS):
        keep, send = back(ext, slot_grads, first if i == 0 else turned, i > 0)
        both = add(keep, swap(send))
        mine, onward = both[:count], both[count : 3 * count]
        passed = flow(both[3 * count :])
        if i < PARTS - 1:
            came = flow(onward)
            mine = (mine, flow(passed))
        else:
            came = flow(jnp.concatenate([onward[:count], add(onward[count:], passed)], axis=0))
            mine = (mine,)
        pieces.append((*mine, came[count:], swap(came[:count])))
    counts = [len(p) for p in pieces]
    pieces = [x for p in pieces for x in p]

    return pl.pallas_call(
        lambda *refs: finish_kernel(counts, *refs),
        in_specs=[VMEM] * (2 + len(pieces)),
        out_specs=VMEM,
        out_shape=jax.ShapeDtypeStruct((count, width), BF16),
        compiler_params=params(),
        name="finish",
    )(hidden, gain.reshape(1, width), *pieces)


def solution(mesh):
    return jax.shard_map(
        on_device,
        mesh=mesh,
        in_specs=(
            P(("dp", "tensor"), None),
            P(),
            P(None, "tensor"),
            P(None, "tensor"),
            P(None, "tensor"),
            P(("dp", "tensor"), None),
            P(("dp", "tensor"), None),
            P(("dp", "tensor")),
            P("dp", None),
        ),
        out_specs=P(("dp", "tensor"), None),
        check_vma=False,
    )
```

```python
import jax
import jax.numpy as jnp
from jax import lax
from jax.experimental import pallas as pl
from jax.experimental.pallas import tpu as pltpu
from jax.sharding import PartitionSpec as P

HD = 128
KC = 16
PARTS = 2
EXT = 128
HEADS_AT = 8192 + EXT
STEP = 1024
PIECES = 4
TURNED = (2, 4)
TURN = 512
EPSILON = 1e-05
BASE = 500000.0
F32 = jnp.float32
BF16 = jnp.bfloat16

TOKEN = jax.ShapeDtypeStruct((8, 128), F32)
VMEM = pl.BlockSpec(memory_space=pltpu.VMEM)
ANY = pl.BlockSpec(memory_space=pl.ANY)


def params(mib=8):
    return pltpu.CompilerParams(vmem_limit_bytes=mib * 2**20)


def in_hbm(x):
    return pltpu.with_memory_space_constraint(x, pltpu.HBM)


def in_vmem(x):
    return pltpu.with_memory_space_constraint(x, pltpu.VMEM)


def dot(a, b, dims):
    return lax.dot_general(a, b, (dims, ((), ())), preferred_element_type=F32)


def iota(shape, axis):
    return lax.broadcasted_iota(jnp.int32, shape, axis)


def chip_and_core():
    here = lax.axis_index("tensor")
    return here // 2, here % 2, lax.axis_size("tensor") // 2


def norm_kernel(hidden_hbm, gain_hbm, owner_hbm, completion_hbm, grad_hbm, leave_ref, cross_ref, next_ref, own_ref, *rest):
    hidden_ref, gain_ref, owner_ref, completion_ref, grad_ref, sems = rest
    copies = [
        pltpu.make_async_copy(src, dst, sems.at[i])
        for i, (src, dst) in enumerate(
            (
                (hidden_hbm, hidden_ref),
                (gain_hbm, gain_ref),
                (owner_hbm, owner_ref),
                (completion_hbm, completion_ref),
                (grad_hbm, grad_ref),
            )
        )
    ]
    for copy in copies:
        copy.start()
    for copy in copies:
        copy.wait()
    count, width = hidden_ref.shape
    wide = hidden_ref[...].astype(F32)
    inverse = lax.rsqrt(jnp.mean(wide * wide, axis=1, keepdims=True) + EPSILON)
    rows, cols = iota((count, count), 0), iota((count, count), 1)
    owner_row = owner_ref[...].astype(F32)
    owner = jnp.sum(jnp.where(rows == cols, owner_row, 0.0), axis=1, keepdims=True)
    label = jnp.sum(
        jnp.where(rows == cols, completion_ref[...].astype(F32) + 1.0, 0.0), axis=1, keepdims=True
    )
    rank = jnp.sum(jnp.where((owner == owner_row) & (cols < rows), 1.0, 0.0), axis=1, keepdims=True)
    here = lax.axis_index("tensor").astype(F32)
    slot = owner * 16.0 + here * 2.0 + rank
    lane = iota((count, EXT), 1)
    ext = jnp.where(lane == 0, slot, jnp.where(lane == 1, label, 0.0)).astype(BF16)
    normed = (wide * inverse * gain_ref[...]).astype(BF16)
    for ref in (leave_ref, cross_ref):
        ref[:, 0:width] = normed
        ref[:, width : width + EXT] = ext
    chip, core, chips = chip_and_core()
    each = own_ref.shape[1]

    def heads(at, n):
        return grad_ref[:, pl.ds(pl.multiple_of(at * each, each), n * each)]

    up, down = (chip + 1) % chips, (chip + chips - 1) % chips
    at = width + EXT
    leave_ref[:, at:] = heads(2 * ((chip + 2) % chips), 2)
    next_ref[...] = heads(2 * jnp.where(core == 0, up, down), 2)
    cross_ref[:, at : at + 2 * each] = heads(2 * jnp.where(core == 0, down, up), 2)
    cross_ref[:, at + 2 * each :] = heads(2 * chip + 1 - core, 1)
    own_ref[...] = heads(2 * chip + core, 1)


def join_kernel(other_ref, next_ref, out_ref):
    n = out_ref.shape[1] - next_ref.shape[1]
    out_ref[:, 0:n] = other_ref[:, 0:n]
    out_ref[:, n:] = next_ref[...]


def half(rows_ref, heads_ref, at, out_ref):
    n = HEADS_AT
    each = out_ref.shape[1] - n
    _, core, _ = chip_and_core()
    out_ref[:, 0:n] = rows_ref[:, 0:n]
    first, second = heads_ref[:, at : at + each], heads_ref[:, at + each : at + 2 * each]
    out_ref[:, n:] = jnp.where(core == 0, second, first)


def half_near_kernel(near_ref, near_o_ref, _, out_ref, out_o_ref):
    each = out_ref.shape[1] - HEADS_AT
    half(near_ref, near_o_ref, HEADS_AT + 2 * each, out_ref)
    half(near_o_ref, near_o_ref, HEADS_AT, out_o_ref)


def half_far_kernel(far_ref, _, out_ref):
    half(far_ref, far_ref, HEADS_AT, out_ref)


def relay_kernel(near_ref, _, out_ref):
    out_ref[...] = near_ref[...]


def load_kernel(part, wq_hbm, wk_hbm, wv_hbm, _, out_ref, token_ref, *rest):
    turned_ref, sems = rest[0], rest[-1]
    token_ref[...] = jnp.zeros_like(token_ref)
    span = out_ref.shape[0]
    step = span // PIECES
    skip = PIECES - turned_ref.shape[1] // step
    copies = []
    for j in range(PIECES):
        at = 0
        for w in (wq_hbm, wk_hbm, wv_hbm):
            n = w.shape[1]
            copies.append(
                pltpu.make_async_copy(
                    w.at[pl.ds(part * span + j * step, step), :],
                    out_ref.at[pl.ds(j * step, step), pl.ds(at, n)],
                    sems.at[len(copies)],
                )
            )
            at += n
    for copy in copies:
        copy.start()
    for j in range(PIECES):
        for copy in copies[3 * j : 3 * j + 3]:
            copy.wait()
        if j < skip:
            continue

        @pl.loop(0, step // TURN)
        def _(k):
            at = pl.ds(pl.multiple_of(j * step + k * TURN, TURN), TURN)
            to = pl.ds(pl.multiple_of((j - skip) * step + k * TURN, TURN), TURN)
            turned_ref[:, to] = jnp.transpose(out_ref[at, :])


def load(part, weights, after):
    span = weights[0].shape[0] // PARTS
    cols = sum(w.shape[1] for w in weights)
    return pl.pallas_call(
        lambda *refs: load_kernel(part, *refs),
        in_specs=[ANY] * 3 + [VMEM],
        out_specs=[VMEM] * 3,
        out_shape=[pltpu.VMEM((span, cols), BF16), TOKEN] + [pltpu.VMEM((cols, span * TURNED[part] // PIECES), BF16)],
        scratch_shapes=[pltpu.SemaphoreType.DMA((3 * PIECES,))],
        compiler_params=params(),
        cost_estimate=pl.CostEstimate(flops=0, bytes_accessed=2 * span * cols, transcendentals=0),
        name="load",
    )(*[in_hbm(w) for w in weights], after)


def project_kernel(count, *refs):
    blocks = refs[:count]
    parts = refs[count : count + PARTS]
    own_ref, out_ref, ext_ref, x_ref = refs[count + PARTS :]
    width = x_ref.shape[1]
    rows = blocks[0].shape[0]
    for i, b in enumerate(blocks):
        x_ref[i * rows : (i + 1) * rows, :] = b[:, 0:width]
    exts = [b[:, width : width + EXT] for b in blocks]
    mine, other, near, near_o, across, across_o, far, far_o = exts
    ext_ref[...] = jnp.concatenate([mine, across, across_o, far, other, near, near_o, far_o], axis=0)
    total = None
    for i, w in enumerate(parts):
        span = w.shape[0]
        value = dot(x_ref[:, i * span : (i + 1) * span], w[...], ((1,), (0,)))
        total = value if total is None else total + value
    total = total.astype(BF16)
    cols = total.shape[1]
    slots = out_ref.shape[0]
    ext = jnp.concatenate(exts, axis=0)
    place = jnp.transpose(ext.astype(F32))[0:1, :]
    spread = (place == iota((slots, ext.shape[0]), 0).astype(F32)).astype(BF16)
    out_ref[:, 0:cols] = dot(spread, total, ((1,), (0,))).astype(BF16)
    out_ref[:, cols : cols + EXT] = dot(spread, ext, ((1,), (0,))).astype(BF16)
    _, core, _ = chip_and_core()
    n = HEADS_AT
    each = own_ref.shape[1]

    def heads(b, at):
        return jnp.where(core == 0, b[:, at : at + each], b[:, at + each : at + 2 * each])

    mine, other, near, near_o, across, across_o, far, far_o = blocks
    grads = [own_ref[...], other[:, n + 2 * each :], heads(near_o, n + 2 * each), heads(near_o, n)]
    grads += [across[:, n:], across_o[:, n:], heads(far, n), far_o[:, n:]]
    out_ref[:, cols + EXT :] = dot(spread, jnp.concatenate(grads, axis=0), ((1,), (0,))).astype(BF16)


def project(blocks, loaded, own, slots):
    rows = sum(b.shape[0] for b in blocks)
    span, cols = loaded[0].shape
    width = span * PARTS
    return pl.pallas_call(
        lambda *refs: project_kernel(len(blocks), *refs),
        in_specs=[VMEM] * (len(blocks) + PARTS + 1),
        out_specs=[VMEM] * 2,
        out_shape=[
            jax.ShapeDtypeStruct((slots, cols + EXT + own.shape[1]), BF16),
            jax.ShapeDtypeStruct((rows, EXT), BF16),
        ],
        scratch_shapes=[pltpu.VMEM((rows, width), BF16)],
        compiler_params=params(),
        cost_estimate=pl.CostEstimate(
            flops=2 * rows * width * cols, bytes_accessed=2 * width * cols, transcendentals=0
        ),
        name="project",
    )(*blocks, *[in_vmem(w) for w in loaded], own)


def attend_kernel(got_ref, rewards_ref, out_ref):
    slots = got_ref.shape[0]
    heads = out_ref.shape[1] // HD - 2
    kcol = heads * HD
    vcol = kcol + HD
    ecol = vcol + HD
    gcol = ecol + EXT
    factor = HD**-0.5
    ext = got_ref[:, ecol : ecol + EXT].astype(F32)
    label = ext[:, 1:2]
    label_row = jnp.transpose(ext)[1:2, :]
    rows, cols = iota((slots, slots), 0), iota((slots, slots), 1)
    same = label == label_row
    bias = jnp.where(same & (rows <= cols), 0.0, -1e30)
    position = jnp.sum(jnp.where(same & (cols < rows), 1.0, 0.0), axis=1, keepdims=True)
    lane = iota((slots, HD), 1)
    half = HD // 2
    index = jnp.where(lane < half, lane, lane - half).astype(F32)
    freq = jnp.exp(index * (-2.0 / HD * jnp.log(F32(BASE))))
    angle = position * freq
    cosine = jnp.cos(angle)
    sine = jnp.sin(angle)
    sine = jnp.where(lane < half, -sine, sine)

    def rope(u):
        return u * cosine + pltpu.roll(u, half, 1) * sine

    def rope_back(u):
        return u * cosine - pltpu.roll(u, half, 1) * sine

    scaled = rewards_ref[...].astype(F32) / 256.0
    advantage = scaled - (jnp.sum(scaled) - scaled) / (KC - 1)
    advantage = jnp.concatenate([advantage, jnp.zeros((1, EXT - KC), F32)], axis=1)
    weight = jnp.sum(jnp.where(label - 1.0 == lane.astype(F32), advantage, 0.0), axis=1, keepdims=True)

    key = rope(got_ref[:, kcol : kcol + HD].astype(F32)).astype(BF16)
    value = got_ref[:, vcol : vcol + HD]
    grad_key = jnp.zeros((slots, HD), F32)
    grad_value = jnp.zeros((slots, HD), F32)
    for h in range(heads):
        at = slice(h * HD, (h + 1) * HD)
        query = rope(got_ref[:, at].astype(F32)).astype(BF16)
        grad = (got_ref[:, gcol + h * HD : gcol + (h + 1) * HD].astype(F32) * weight).astype(BF16)
        scores = dot(key, query, ((1,), (1,))) * factor + bias
        highest = jnp.max(scores, axis=0, keepdims=True)
        weights = jnp.exp(scores - highest)
        probs = weights * (1.0 / jnp.sum(weights, axis=0, keepdims=True))
        grad_value = grad_value + dot(probs.astype(BF16), grad, ((1,), (0,)))
        grad_probs = dot(value, grad, ((1,), (1,)))
        inner = jnp.sum(probs * grad_probs, axis=0, keepdims=True)
        grad_scores = (probs * (grad_probs - inner) * factor).astype(BF16)
        grad_query = dot(grad_scores, key, ((0,), (0,)))
        grad_key = grad_key + dot(grad_scores, query, ((1,), (0,)))
        out_ref[:, at] = rope_back(grad_query).astype(BF16)
    out_ref[:, kcol : kcol + HD] = rope_back(grad_key).astype(BF16)
    out_ref[:, vcol : vcol + HD] = grad_value.astype(BF16)


def back_kernel(ext_ref, slots_ref, *refs):
    weights, (keep_ref, send_ref) = refs[:-2], refs[-2:]
    half_rows, span = keep_ref.shape
    slots = slots_ref.shape[0]
    hot = (ext_ref[:, 0:1].astype(F32) == iota((ext_ref.shape[0], slots), 1).astype(F32)).astype(BF16)
    held = dot(hot, slots_ref[...], ((1,), (0,))).astype(BF16)
    turned_ref = weights[-1]
    plain = span - turned_ref.shape[1]
    for j in range(span // STEP):
        at = slice(j * STEP, (j + 1) * STEP)
        if j * STEP < plain:
            term = dot(held, weights[0][at, :], ((1,), (1,)))
        else:
            term = dot(held, turned_ref[:, j * STEP - plain : (j + 1) * STEP - plain], ((1,), (0,)))
        term = term.astype(BF16)
        keep_ref[:, at] = term[0:half_rows]
        send_ref[:, at] = term[half_rows:]


def back(ext, slot_grads, w, turned):
    rows = ext.shape[0]
    cols = turned.shape[0]
    span = turned.shape[1] if w is None else w.shape[0]
    weights = [in_vmem(x) for x in (w, turned) if x is not None]
    out = jax.ShapeDtypeStruct((rows // 2, span), BF16)
    return pl.pallas_call(
        back_kernel,
        in_specs=[VMEM] * (2 + len(weights)),
        out_specs=[VMEM] * 2,
        out_shape=[out, out],
        compiler_params=params(),
        cost_estimate=pl.CostEstimate(
            flops=2 * rows * span * cols, bytes_accessed=2 * span * cols, transcendentals=0
        ),
        name="back",
    )(ext, slot_grads, *weights)


def finish_kernel(counts, hidden_ref, gain_ref, *refs):
    out_ref = refs[-1]
    wide = hidden_ref[...].astype(F32)
    inverse = lax.rsqrt(jnp.mean(wide * wide, axis=1, keepdims=True) + EPSILON)
    parts = []
    at = 0
    for n in counts:
        parts.append(sum(ref[...].astype(F32) for ref in refs[at : at + n]))
        at += n
    scaled = jnp.concatenate(parts, axis=1) * gain_ref[...]
    inner = jnp.mean(scaled * wide, axis=1, keepdims=True)
    out_ref[...] = (inverse * scaled - wide * inverse * inverse * inverse * inner).astype(BF16)


def on_device(hidden, gain, w_query, w_key, w_value, out_grad, owner, completion, rewards):
    groups = lax.axis_size("dp")
    ranks = lax.axis_size("tensor")
    chips = ranks // 2
    count, width = hidden.shape
    query_cols = w_query.shape[1]
    slots = 2 * groups * ranks
    span = width // PARTS

    swap_pairs = [(t, t ^ 1) for t in range(ranks)]
    flow_pairs = [(t, (t // 2 + (1 if t % 2 == 0 else chips - 1)) % chips * 2 + t % 2) for t in range(ranks)]

    def swap(x):
        return lax.ppermute(x, "tensor", swap_pairs)

    def flow(x):
        return lax.ppermute(x, "tensor", flow_pairs)

    near_cols = HEADS_AT + 2 * query_cols

    def rows_of(cols):
        return jax.ShapeDtypeStruct((count, cols), BF16)

    leave, cross, onto_next, own = pl.pallas_call(
        norm_kernel,
        in_specs=[ANY] * 5,
        out_specs=[VMEM] * 4,
        out_shape=[rows_of(n) for n in (near_cols, near_cols + query_cols, 2 * query_cols, query_cols)],
        scratch_shapes=[
            pltpu.VMEM((count, width), BF16),
            pltpu.VMEM((1, width), F32),
            pltpu.VMEM((1, count), jnp.int32),
            pltpu.VMEM((1, count), jnp.int32),
            pltpu.VMEM((count, width), BF16),
            pltpu.SemaphoreType.DMA((5,)),
        ],
        compiler_params=params(),
        name="norm",
    )(
        *[
            in_hbm(x)
            for x in (hidden, gain.reshape(1, width), owner.reshape(1, count), completion.reshape(1, count), out_grad)
        ]
    )
    near = flow(leave)
    other = swap(cross)
    leave_o = pl.pallas_call(
        join_kernel,
        in_specs=[VMEM] * 2,
        out_specs=VMEM,
        out_shape=rows_of(near_cols + 2 * query_cols),
        compiler_params=params(),
        name="join",
    )(other, onto_next)

    weights = (w_query, w_key, w_value)
    near_o = flow(leave_o)
    first, ready, first_turned = load(0, weights, leave_o)
    passed = pl.pallas_call(
        relay_kernel,
        in_specs=[VMEM] * 2,
        out_specs=VMEM,
        out_shape=rows_of(near_cols),
        compiler_params=params(),
        name="relay",
    )(near, ready)
    far = flow(passed)
    second, ready_too, second_turned = load(1, weights, passed)

    half_rows = rows_of(HEADS_AT + query_cols)
    half_near, half_near_o = pl.pallas_call(
        half_near_kernel,
        in_specs=[VMEM] * 3,
        out_specs=[VMEM] * 2,
        out_shape=[half_rows] * 2,
        compiler_params=params(),
        name="half_near",
    )(near, near_o, ready_too)
    half_far = pl.pallas_call(
        half_far_kernel,
        in_specs=[VMEM] * 2,
        out_specs=VMEM,
        out_shape=half_rows,
        compiler_params=params(),
        name="half_far",
    )(far, ready_too)
    blocks = (leave, other, near, near_o, swap(half_near), swap(half_near_o), far, swap(half_far))
    loaded = (first, second)
    total, ext = project(blocks, loaded, own, slots)
    got = lax.all_to_all(
        total.reshape(groups, 2 * ranks, total.shape[1]), "dp", split_axis=0, concat_axis=0, tiled=True
    ).reshape(total.shape)

    cols = sum(w.shape[1] for w in weights)
    grads = pl.pallas_call(
        attend_kernel,
        in_specs=[VMEM] * 2,
        out_specs=VMEM,
        out_shape=jax.ShapeDtypeStruct((slots, cols), BF16),
        compiler_params=params(),
        name="attend",
    )(got, rewards)
    slot_grads = lax.all_to_all(
        grads.reshape(groups, 2 * ranks, cols), "dp", split_axis=0, concat_axis=0, tiled=True
    ).reshape(grads.shape)

    def add(a, b):
        return (a.astype(F32) + b.astype(F32)).astype(BF16)

    pieces = []
    for i in range(PARTS):
        keep, send = back(ext, slot_grads, *((first, first_turned) if i == 0 else (None, second_turned)))
        both = add(keep, swap(send))
        mine, onward = both[:count], both[count : 3 * count]
        passed = flow(both[3 * count :])
        if i < PARTS - 1:
            came = flow(onward)
            mine = (mine, flow(passed))
        else:
            came = flow(jnp.concatenate([onward[:count], add(onward[count:], passed)], axis=0))
            mine = (mine,)
        pieces.append((*mine, came[count:], swap(came[:count])))
    counts = [len(p) for p in pieces]
    pieces = [x for p in pieces for x in p]

    return pl.pallas_call(
        lambda *refs: finish_kernel(counts, *refs),
        in_specs=[VMEM] * (2 + len(pieces)),
        out_specs=VMEM,
        out_shape=jax.ShapeDtypeStruct((count, width), BF16),
        compiler_params=params(),
        name="finish",
    )(hidden, gain.reshape(1, width), *pieces)


def solution(mesh):
    return jax.shard_map(
        on_device,
        mesh=mesh,
        in_specs=(
            P(("dp", "tensor"), None),
            P(),
            P(None, "tensor"),
            P(None, "tensor"),
            P(None, "tensor"),
            P(("dp", "tensor"), None),
            P(("dp", "tensor"), None),
            P(("dp", "tensor")),
            P("dp", None),
        ),
        out_specs=P(("dp", "tensor"), None),
        check_vma=False,
    )
```

```python
import jax
import jax.numpy as jnp
from jax import lax
from jax.experimental import pallas as pl
from jax.experimental.pallas import tpu as pltpu
from jax.sharding import PartitionSpec as P

HD = 128
KC = 16
PARTS = 2
EXT = 128
HEADS_AT = 8192 + EXT
STEP = 1024
PIECES = 4
TURNED = (3, 4)
TURN = 512
EPSILON = 1e-05
BASE = 500000.0
F32 = jnp.float32
BF16 = jnp.bfloat16

TOKEN = jax.ShapeDtypeStruct((8, 128), F32)
VMEM = pl.BlockSpec(memory_space=pltpu.VMEM)
ANY = pl.BlockSpec(memory_space=pl.ANY)


def params(mib=8):
    return pltpu.CompilerParams(vmem_limit_bytes=mib * 2**20)


def in_hbm(x):
    return pltpu.with_memory_space_constraint(x, pltpu.HBM)


def in_vmem(x):
    return pltpu.with_memory_space_constraint(x, pltpu.VMEM)


def dot(a, b, dims):
    return lax.dot_general(a, b, (dims, ((), ())), preferred_element_type=F32)


def iota(shape, axis):
    return lax.broadcasted_iota(jnp.int32, shape, axis)


def chip_and_core():
    here = lax.axis_index("tensor")
    return here // 2, here % 2, lax.axis_size("tensor") // 2


def norm_kernel(hidden_hbm, gain_hbm, owner_hbm, completion_hbm, grad_hbm, leave_ref, cross_ref, next_ref, own_ref, *rest):
    hidden_ref, gain_ref, owner_ref, completion_ref, grad_ref, sems = rest
    copies = [
        pltpu.make_async_copy(src, dst, sems.at[i])
        for i, (src, dst) in enumerate(
            (
                (hidden_hbm, hidden_ref),
                (gain_hbm, gain_ref),
                (owner_hbm, owner_ref),
                (completion_hbm, completion_ref),
                (grad_hbm, grad_ref),
            )
        )
    ]
    for copy in copies:
        copy.start()
    for copy in copies:
        copy.wait()
    count, width = hidden_ref.shape
    wide = hidden_ref[...].astype(F32)
    inverse = lax.rsqrt(jnp.mean(wide * wide, axis=1, keepdims=True) + EPSILON)
    rows, cols = iota((count, count), 0), iota((count, count), 1)
    owner_row = owner_ref[...].astype(F32)
    owner = jnp.sum(jnp.where(rows == cols, owner_row, 0.0), axis=1, keepdims=True)
    label = jnp.sum(
        jnp.where(rows == cols, completion_ref[...].astype(F32) + 1.0, 0.0), axis=1, keepdims=True
    )
    rank = jnp.sum(jnp.where((owner == owner_row) & (cols < rows), 1.0, 0.0), axis=1, keepdims=True)
    here = lax.axis_index("tensor").astype(F32)
    slot = owner * 16.0 + here * 2.0 + rank
    lane = iota((count, EXT), 1)
    ext = jnp.where(lane == 0, slot, jnp.where(lane == 1, label, 0.0)).astype(BF16)
    normed = (wide * inverse * gain_ref[...]).astype(BF16)
    for ref in (leave_ref, cross_ref):
        ref[:, 0:width] = normed
        ref[:, width : width + EXT] = ext
    chip, core, chips = chip_and_core()
    each = own_ref.shape[1]

    def heads(at, n):
        return grad_ref[:, pl.ds(pl.multiple_of(at * each, each), n * each)]

    up, down = (chip + 1) % chips, (chip + chips - 1) % chips
    at = width + EXT
    leave_ref[:, at:] = heads(2 * ((chip + 2) % chips), 2)
    next_ref[...] = heads(2 * jnp.where(core == 0, up, down), 2)
    cross_ref[:, at : at + 2 * each] = heads(2 * jnp.where(core == 0, down, up), 2)
    cross_ref[:, at + 2 * each :] = heads(2 * chip + 1 - core, 1)
    own_ref[...] = heads(2 * chip + core, 1)


def join_kernel(other_ref, next_ref, out_ref):
    n = out_ref.shape[1] - next_ref.shape[1]
    out_ref[:, 0:n] = other_ref[:, 0:n]
    out_ref[:, n:] = next_ref[...]


def half(rows_ref, heads_ref, at, out_ref):
    n = HEADS_AT
    each = out_ref.shape[1] - n
    _, core, _ = chip_and_core()
    out_ref[:, 0:n] = rows_ref[:, 0:n]
    first, second = heads_ref[:, at : at + each], heads_ref[:, at + each : at + 2 * each]
    out_ref[:, n:] = jnp.where(core == 0, second, first)


def half_near_kernel(near_ref, near_o_ref, _, out_ref, out_o_ref):
    each = out_ref.shape[1] - HEADS_AT
    half(near_ref, near_o_ref, HEADS_AT + 2 * each, out_ref)
    half(near_o_ref, near_o_ref, HEADS_AT, out_o_ref)


def half_far_kernel(far_ref, _, out_ref):
    half(far_ref, far_ref, HEADS_AT, out_ref)


def relay_kernel(near_ref, _, out_ref):
    out_ref[...] = near_ref[...]


def load_kernel(part, wq_hbm, wk_hbm, wv_hbm, _, out_ref, token_ref, *rest):
    turned_ref, sems = rest[0], rest[-1]
    token_ref[...] = jnp.zeros_like(token_ref)
    span = out_ref.shape[0]
    step = span // PIECES
    skip = PIECES - turned_ref.shape[1] // step
    copies = []
    for j in range(PIECES):
        at = 0
        for w in (wq_hbm, wk_hbm, wv_hbm):
            n = w.shape[1]
            copies.append(
                pltpu.make_async_copy(
                    w.at[pl.ds(part * span + j * step, step), :],
                    out_ref.at[pl.ds(j * step, step), pl.ds(at, n)],
                    sems.at[len(copies)],
                )
            )
            at += n
    for copy in copies:
        copy.start()
    for j in range(PIECES):
        for copy in copies[3 * j : 3 * j + 3]:
            copy.wait()
        if j < skip:
            continue

        @pl.loop(0, step // TURN)
        def _(k):
            at = pl.ds(pl.multiple_of(j * step + k * TURN, TURN), TURN)
            to = pl.ds(pl.multiple_of((j - skip) * step + k * TURN, TURN), TURN)
            turned_ref[:, to] = jnp.transpose(out_ref[at, :])


def load(part, weights, after):
    span = weights[0].shape[0] // PARTS
    cols = sum(w.shape[1] for w in weights)
    return pl.pallas_call(
        lambda *refs: load_kernel(part, *refs),
        in_specs=[ANY] * 3 + [VMEM],
        out_specs=[VMEM] * 3,
        out_shape=[pltpu.VMEM((span, cols), BF16), TOKEN] + [pltpu.VMEM((cols, span * TURNED[part] // PIECES), BF16)],
        scratch_shapes=[pltpu.SemaphoreType.DMA((3 * PIECES,))],
        compiler_params=params(),
        cost_estimate=pl.CostEstimate(flops=0, bytes_accessed=2 * span * cols, transcendentals=0),
        name="load",
    )(*[in_hbm(w) for w in weights], after)


def project_kernel(count, *refs):
    blocks = refs[:count]
    parts = refs[count : count + PARTS]
    own_ref, out_ref, ext_ref, x_ref = refs[count + PARTS :]
    width = x_ref.shape[1]
    rows = blocks[0].shape[0]
    for i, b in enumerate(blocks):
        x_ref[i * rows : (i + 1) * rows, :] = b[:, 0:width]
    exts = [b[:, width : width + EXT] for b in blocks]
    mine, other, near, near_o, across, across_o, far, far_o = exts
    ext_ref[...] = jnp.concatenate([mine, across, across_o, far, other, near, near_o, far_o], axis=0)
    total = None
    for i, w in enumerate(parts):
        span = w.shape[0]
        value = dot(x_ref[:, i * span : (i + 1) * span], w[...], ((1,), (0,)))
        total = value if total is None else total + value
    total = total.astype(BF16)
    cols = total.shape[1]
    slots = out_ref.shape[0]
    ext = jnp.concatenate(exts, axis=0)
    place = jnp.transpose(ext.astype(F32))[0:1, :]
    spread = (place == iota((slots, ext.shape[0]), 0).astype(F32)).astype(BF16)
    out_ref[:, 0:cols] = dot(spread, total, ((1,), (0,))).astype(BF16)
    out_ref[:, cols : cols + EXT] = dot(spread, ext, ((1,), (0,))).astype(BF16)
    _, core, _ = chip_and_core()
    n = HEADS_AT
    each = own_ref.shape[1]

    def heads(b, at):
        return jnp.where(core == 0, b[:, at : at + each], b[:, at + each : at + 2 * each])

    mine, other, near, near_o, across, across_o, far, far_o = blocks
    grads = [own_ref[...], other[:, n + 2 * each :], heads(near_o, n + 2 * each), heads(near_o, n)]
    grads += [across[:, n:], across_o[:, n:], heads(far, n), far_o[:, n:]]
    out_ref[:, cols + EXT :] = dot(spread, jnp.concatenate(grads, axis=0), ((1,), (0,))).astype(BF16)


def project(blocks, loaded, own, slots):
    rows = sum(b.shape[0] for b in blocks)
    span, cols = loaded[0].shape
    width = span * PARTS
    return pl.pallas_call(
        lambda *refs: project_kernel(len(blocks), *refs),
        in_specs=[VMEM] * (len(blocks) + PARTS + 1),
        out_specs=[VMEM] * 2,
        out_shape=[
            jax.ShapeDtypeStruct((slots, cols + EXT + own.shape[1]), BF16),
            jax.ShapeDtypeStruct((rows, EXT), BF16),
        ],
        scratch_shapes=[pltpu.VMEM((rows, width), BF16)],
        compiler_params=params(),
        cost_estimate=pl.CostEstimate(
            flops=2 * rows * width * cols, bytes_accessed=2 * width * cols, transcendentals=0
        ),
        name="project",
    )(*blocks, *[in_vmem(w) for w in loaded], own)


def attend_kernel(got_ref, rewards_ref, out_ref):
    slots = got_ref.shape[0]
    heads = out_ref.shape[1] // HD - 2
    kcol = heads * HD
    vcol = kcol + HD
    ecol = vcol + HD
    gcol = ecol + EXT
    factor = HD**-0.5
    ext = got_ref[:, ecol : ecol + EXT].astype(F32)
    label = ext[:, 1:2]
    label_row = jnp.transpose(ext)[1:2, :]
    rows, cols = iota((slots, slots), 0), iota((slots, slots), 1)
    same = label == label_row
    bias = jnp.where(same & (rows <= cols), 0.0, -1e30)
    position = jnp.sum(jnp.where(same & (cols < rows), 1.0, 0.0), axis=1, keepdims=True)
    lane = iota((slots, HD), 1)
    half = HD // 2
    index = jnp.where(lane < half, lane, lane - half).astype(F32)
    freq = jnp.exp(index * (-2.0 / HD * jnp.log(F32(BASE))))
    angle = position * freq
    cosine = jnp.cos(angle)
    sine = jnp.sin(angle)
    sine = jnp.where(lane < half, -sine, sine)

    def rope(u):
        return u * cosine + pltpu.roll(u, half, 1) * sine

    def rope_back(u):
        return u * cosine - pltpu.roll(u, half, 1) * sine

    scaled = rewards_ref[...].astype(F32) / 256.0
    advantage = scaled - (jnp.sum(scaled) - scaled) / (KC - 1)
    advantage = jnp.concatenate([advantage, jnp.zeros((1, EXT - KC), F32)], axis=1)
    weight = jnp.sum(jnp.where(label - 1.0 == lane.astype(F32), advantage, 0.0), axis=1, keepdims=True)

    key = rope(got_ref[:, kcol : kcol + HD].astype(F32)).astype(BF16)
    value = got_ref[:, vcol : vcol + HD]
    grad_key = jnp.zeros((slots, HD), F32)
    grad_value = jnp.zeros((slots, HD), F32)
    for h in range(heads):
        at = slice(h * HD, (h + 1) * HD)
        query = rope(got_ref[:, at].astype(F32)).astype(BF16)
        grad = (got_ref[:, gcol + h * HD : gcol + (h + 1) * HD].astype(F32) * weight).astype(BF16)
        scores = dot(key, query, ((1,), (1,))) * factor + bias
        highest = jnp.max(scores, axis=0, keepdims=True)
        weights = jnp.exp(scores - highest)
        probs = weights * (1.0 / jnp.sum(weights, axis=0, keepdims=True))
        grad_value = grad_value + dot(probs.astype(BF16), grad, ((1,), (0,)))
        grad_probs = dot(value, grad, ((1,), (1,)))
        inner = jnp.sum(probs * grad_probs, axis=0, keepdims=True)
        grad_scores = (probs * (grad_probs - inner) * factor).astype(BF16)
        grad_query = dot(grad_scores, key, ((0,), (0,)))
        grad_key = grad_key + dot(grad_scores, query, ((1,), (0,)))
        out_ref[:, at] = rope_back(grad_query).astype(BF16)
    out_ref[:, kcol : kcol + HD] = rope_back(grad_key).astype(BF16)
    out_ref[:, vcol : vcol + HD] = grad_value.astype(BF16)


def back_kernel(ext_ref, slots_ref, *refs):
    weights, (keep_ref, send_ref) = refs[:-2], refs[-2:]
    half_rows, span = keep_ref.shape
    slots = slots_ref.shape[0]
    hot = (ext_ref[:, 0:1].astype(F32) == iota((ext_ref.shape[0], slots), 1).astype(F32)).astype(BF16)
    held = dot(hot, slots_ref[...], ((1,), (0,))).astype(BF16)
    turned_ref = weights[-1]
    plain = span - turned_ref.shape[1]
    for j in range(span // STEP):
        at = slice(j * STEP, (j + 1) * STEP)
        if j * STEP < plain:
            term = dot(held, weights[0][at, :], ((1,), (1,)))
        else:
            term = dot(held, turned_ref[:, j * STEP - plain : (j + 1) * STEP - plain], ((1,), (0,)))
        term = term.astype(BF16)
        keep_ref[:, at] = term[0:half_rows]
        send_ref[:, at] = term[half_rows:]


def back(ext, slot_grads, w, turned):
    rows = ext.shape[0]
    cols = turned.shape[0]
    span = turned.shape[1] if w is None else w.shape[0]
    weights = [in_vmem(x) for x in (w, turned) if x is not None]
    out = jax.ShapeDtypeStruct((rows // 2, span), BF16)
    return pl.pallas_call(
        back_kernel,
        in_specs=[VMEM] * (2 + len(weights)),
        out_specs=[VMEM] * 2,
        out_shape=[out, out],
        compiler_params=params(),
        cost_estimate=pl.CostEstimate(
            flops=2 * rows * span * cols, bytes_accessed=2 * span * cols, transcendentals=0
        ),
        name="back",
    )(ext, slot_grads, *weights)


def finish_kernel(counts, hidden_ref, gain_ref, *refs):
    out_ref = refs[-1]
    wide = hidden_ref[...].astype(F32)
    inverse = lax.rsqrt(jnp.mean(wide * wide, axis=1, keepdims=True) + EPSILON)
    parts = []
    at = 0
    for n in counts:
        parts.append(sum(ref[...].astype(F32) for ref in refs[at : at + n]))
        at += n
    scaled = jnp.concatenate(parts, axis=1) * gain_ref[...]
    inner = jnp.mean(scaled * wide, axis=1, keepdims=True)
    out_ref[...] = (inverse * scaled - wide * inverse * inverse * inverse * inner).astype(BF16)


def on_device(hidden, gain, w_query, w_key, w_value, out_grad, owner, completion, rewards):
    groups = lax.axis_size("dp")
    ranks = lax.axis_size("tensor")
    chips = ranks // 2
    count, width = hidden.shape
    query_cols = w_query.shape[1]
    slots = 2 * groups * ranks
    span = width // PARTS

    swap_pairs = [(t, t ^ 1) for t in range(ranks)]
    flow_pairs = [(t, (t // 2 + (1 if t % 2 == 0 else chips - 1)) % chips * 2 + t % 2) for t in range(ranks)]

    def swap(x):
        return lax.ppermute(x, "tensor", swap_pairs)

    def flow(x):
        return lax.ppermute(x, "tensor", flow_pairs)

    near_cols = HEADS_AT + 2 * query_cols

    def rows_of(cols):
        return jax.ShapeDtypeStruct((count, cols), BF16)

    leave, cross, onto_next, own = pl.pallas_call(
        norm_kernel,
        in_specs=[ANY] * 5,
        out_specs=[VMEM] * 4,
        out_shape=[rows_of(n) for n in (near_cols, near_cols + query_cols, 2 * query_cols, query_cols)],
        scratch_shapes=[
            pltpu.VMEM((count, width), BF16),
            pltpu.VMEM((1, width), F32),
            pltpu.VMEM((1, count), jnp.int32),
            pltpu.VMEM((1, count), jnp.int32),
            pltpu.VMEM((count, width), BF16),
            pltpu.SemaphoreType.DMA((5,)),
        ],
        compiler_params=params(),
        name="norm",
    )(
        *[
            in_hbm(x)
            for x in (hidden, gain.reshape(1, width), owner.reshape(1, count), completion.reshape(1, count), out_grad)
        ]
    )
    near = flow(leave)
    other = swap(cross)
    leave_o = pl.pallas_call(
        join_kernel,
        in_specs=[VMEM] * 2,
        out_specs=VMEM,
        out_shape=rows_of(near_cols + 2 * query_cols),
        compiler_params=params(),
        name="join",
    )(other, onto_next)

    weights = (w_query, w_key, w_value)
    near_o = flow(leave_o)
    first, ready, first_turned = load(0, weights, leave_o)
    passed = pl.pallas_call(
        relay_kernel,
        in_specs=[VMEM] * 2,
        out_specs=VMEM,
        out_shape=rows_of(near_cols),
        compiler_params=params(),
        name="relay",
    )(near, ready)
    far = flow(passed)
    second, ready_too, second_turned = load(1, weights, passed)

    half_rows = rows_of(HEADS_AT + query_cols)
    half_near, half_near_o = pl.pallas_call(
        half_near_kernel,
        in_specs=[VMEM] * 3,
        out_specs=[VMEM] * 2,
        out_shape=[half_rows] * 2,
        compiler_params=params(),
        name="half_near",
    )(near, near_o, ready_too)
    half_far = pl.pallas_call(
        half_far_kernel,
        in_specs=[VMEM] * 2,
        out_specs=VMEM,
        out_shape=half_rows,
        compiler_params=params(),
        name="half_far",
    )(far, ready_too)
    blocks = (leave, other, near, near_o, swap(half_near), swap(half_near_o), far, swap(half_far))
    loaded = (first, second)
    total, ext = project(blocks, loaded, own, slots)
    got = lax.all_to_all(
        total.reshape(groups, 2 * ranks, total.shape[1]), "dp", split_axis=0, concat_axis=0, tiled=True
    ).reshape(total.shape)

    cols = sum(w.shape[1] for w in weights)
    grads = pl.pallas_call(
        attend_kernel,
        in_specs=[VMEM] * 2,
        out_specs=VMEM,
        out_shape=jax.ShapeDtypeStruct((slots, cols), BF16),
        compiler_params=params(),
        name="attend",
    )(got, rewards)
    slot_grads = lax.all_to_all(
        grads.reshape(groups, 2 * ranks, cols), "dp", split_axis=0, concat_axis=0, tiled=True
    ).reshape(grads.shape)

    def add(a, b):
        return (a.astype(F32) + b.astype(F32)).astype(BF16)

    pieces = []
    for i in range(PARTS):
        keep, send = back(ext, slot_grads, *((first, first_turned) if i == 0 else (None, second_turned)))
        both = add(keep, swap(send))
        mine, onward = both[:count], both[count : 3 * count]
        passed = flow(both[3 * count :])
        if i < PARTS - 1:
            came = flow(onward)
            mine = (mine, flow(passed))
        else:
            came = flow(jnp.concatenate([onward[:count], add(onward[count:], passed)], axis=0))
            mine = (mine,)
        pieces.append((*mine, came[count:], swap(came[:count])))
    counts = [len(p) for p in pieces]
    pieces = [x for p in pieces for x in p]

    return pl.pallas_call(
        lambda *refs: finish_kernel(counts, *refs),
        in_specs=[VMEM] * (2 + len(pieces)),
        out_specs=VMEM,
        out_shape=jax.ShapeDtypeStruct((count, width), BF16),
        compiler_params=params(),
        name="finish",
    )(hidden, gain.reshape(1, width), *pieces)


def solution(mesh):
    return jax.shard_map(
        on_device,
        mesh=mesh,
        in_specs=(
            P(("dp", "tensor"), None),
            P(),
            P(None, "tensor"),
            P(None, "tensor"),
            P(None, "tensor"),
            P(("dp", "tensor"), None),
            P(("dp", "tensor"), None),
            P(("dp", "tensor")),
            P("dp", None),
        ),
        out_specs=P(("dp", "tensor"), None),
        check_vma=False,
    )
```
